32 devices in a mesh: tensor: 4 (over y, x), seq: 4 (over z), dp: 2 (over core).
Axes of the slice: x: 2, y: 2, z: 4, core: 2. Of those that a mesh axis runs over, the one named last changes fastest.
Arguments:
- residual_in: bfloat16 [8, 2048, 1536], P('dp', 'seq'), may hold values from -6 to 6
- lengths: int32 [8], P('dp'), may hold values from 512 to 2048, as said below
- input_gain: float32 [1536], replicated, may hold values from 0.5 to 1.5
- main_in_weight: bfloat16 [1536, 2, 3072], P(None, None, 'tensor'), may hold values from -0.15625 to 0.15625
- weight_shared: bfloat16 [1536, 256], replicated, may hold values from -0.15625 to 0.15625
- step_in_weight: bfloat16 [1536, 48], P(None, 'tensor'), may hold values from -0.0390625 to 0.0390625
- filter_main: float32 [5, 3072], P(None, 'tensor'), may hold values from -3 to 3
- filter_shared: float32 [5, 256], replicated, may hold values from -3 to 3
- head_terms: float32 [3, 48], P(None, 'tensor'), may hold values from -12 to 2
- output_gain: float32 [3072], P('tensor'), may hold values from 0.5 to 1.5
- out_projection_weight: bfloat16 [3072, 1536], P('tensor'), may hold values from -0.109375 to 0.109375
- cotangent: bfloat16 [8, 2048, 1536], P('dp', 'seq'), may hold values from -6 to 6
Outputs:
- block_out: bfloat16 [8, 2048, 1536], P('dp', 'seq')
- input_grad: bfloat16 [8, 2048, 1536], P('dp', 'seq')
- grad_input_gain: float32 [1536], replicated
- grad_weight_main: float32 [1536, 2, 3072], P(('seq', 'dp'), None, 'tensor')
- grad_weight_shared: float32 [1536, 256], P(('seq', 'dp'))
- grad_weight_step: float32 [1536, 48], P(('seq', 'dp'), 'tensor')
- grad_filter_main: float32 [5, 3072], P(None, 'tensor')
- grad_filter_shared: float32 [5, 256], replicated
- grad_head_terms: float32 [3, 48], P(None, 'tensor')
- grad_output_gain: float32 [3072], P('tensor')
- grad_weight_out: float32 [3072, 1536], P('tensor', ('seq', 'dp'))
The draws below stay inside these ranges and needn't reach their ends.
Inputs may be any that keep to these rules, and one draw needn't show every extreme that they name: `lengths`: in each aligned group of 4 sequences (those of one index of dp) one sequence has length 2048.
All inputs are finite; a program needn't handle non-finite values.
Results may differ from the reference program's by a relative error of at most 0.0088.
Values may be sent and summed in bfloat16 or wider, within the bound.
No kernel may reach another device: no remote copies, remote signals or barrier semaphores. Data moves between devices by JAX's collectives and lax.ppermute only.
A program may use at most 256 MiB of HBM per device.

```python
import jax
import jax.numpy as jnp
from jax import lax

D = 1536
HEADS = 48
HEADDIM = 64
STATE = 128
CONV = 4
BLOCK_LEN = 256
SEQS_DEV = 4
INNER = 3072
LEN = 2048
SEQS = 8


def draw_lengths(key, part):
    key = jax.random.fold_in(key, 3)
    first, second = jax.random.split(key)
    sizes = jax.random.randint(first, (SEQS,), LEN // 4, LEN + 1)
    groups = SEQS // SEQS_DEV
    chosen = jax.random.randint(second, (groups,), 0, SEQS_DEV)
    slot = jnp.arange(SEQS) % SEQS_DEV
    full = slot == jnp.repeat(chosen, SEQS_DEV)
    return jnp.where(full, LEN, sizes).astype(jnp.int32)


def draw_head_terms(key, part):
    key = jax.random.fold_in(key, 7)
    first, second, third = jax.random.split(key, 3)
    step = jnp.exp(jax.random.uniform(first, (HEADS,), jnp.float32, jnp.log(0.01), jnp.log(0.1)))
    bias = jnp.log(jnp.expm1(step))
    rate = jnp.exp(jax.random.uniform(second, (HEADS,), jnp.float32, jnp.log(0.25 / LEN), jnp.log(1.0 / 30.0)))
    skip = jax.random.uniform(third, (HEADS,), jnp.float32, 0.5, 1.5)
    return jnp.stack([bias, jnp.log(rate / step), skip]).astype(jnp.float32)


def steps_of(stream_key, dims, cuts, least, top_value):
    factor_of, own = 1.0, jax.random.fold_in(stream_key, 6)
    for axis_at, parts in cuts:
        draws = jnp.exp(jax.random.uniform(jax.random.fold_in(own, axis_at), (parts,), jnp.float32, least / len(cuts), top_value / len(cuts)))
        factor_of = factor_of * jnp.repeat(draws, dims[axis_at] // parts).reshape([-1 if axis == axis_at else 1 for axis in range(len(dims))])
    return factor_of


def centred(stream_key, shape, deviation, most, shards=(), held_as=jnp.bfloat16):
    values = deviation * jax.random.normal(stream_key, shape, jnp.float32)
    if shards:
        values = values * steps_of(stream_key, shape, shards, -0.22, 0.18)
    return jnp.clip(values, -most, most).astype(held_as)


def setup_inputs(seed: int = 0) -> dict:
    keys = jax.random.split(jax.random.key(seed), 13)
    return {
        "residual_in": centred(keys[0], (SEQS, LEN, D), 1.0, 6.0, ((0, 2), (1, 4))),
        "lengths": draw_lengths(jax.random.fold_in(keys[12], 71), 0),
        "input_gain": jnp.clip(1.0 + 0.1 * jax.random.normal(keys[2], (D,), jnp.float32), 0.5, 1.5),
        "main_in_weight": centred(keys[3], (D, 2, INNER), D ** -0.5, 0.15625, ((2, 4),)),
        "weight_shared": centred(keys[4], (D, 2 * STATE), D ** -0.5, 0.15625),
        "step_in_weight": centred(keys[5], (D, HEADS), (16 * D) ** -0.5, 0.0390625, ((1, 4),)),
        "filter_main": centred(keys[6], (CONV + 1, INNER), 0.5, 3.0, ((1, 4),), jnp.float32),
        "filter_shared": centred(keys[7], (CONV + 1, 2 * STATE), 0.5, 3.0, (), jnp.float32),
        "head_terms": draw_head_terms(jax.random.fold_in(keys[12], 71), 0),
        "output_gain": jnp.clip(1.0 + 0.1 * jax.random.normal(keys[9], (INNER,), jnp.float32), 0.5, 1.5),
        "out_projection_weight": centred(keys[10], (INNER, D), INNER ** -0.5, 0.109375, ((0, 4),)),
        "cotangent": centred(keys[11], (SEQS, LEN, D), 1.0, 6.0, ((0, 2), (1, 4))),
    }


EPSILON = 1e-05
PRECISE_MODE = lax.Precision.HIGHEST

@jax.custom_vjp
def reduced_width(v):
    return lax.optimization_barrier(v.astype(jnp.bfloat16)).astype(jnp.float32)

@jax.custom_vjp
def reduced_width_back(v):
    return v

def low_keep(v):
    return (reduced_width(v), None)

def low_pass(kept, grad):
    return (grad,)

def back_keep(v):
    return (v, None)

def back_low(kept, grad):
    return (reduced_width(grad),)
reduced_width.defvjp(low_keep, low_pass)
reduced_width_back.defvjp(back_keep, back_low)

def block_step(carry_state, pieces):
    values, step_size, log_decay, inject, readout = pieces
    running = jnp.cumsum(log_decay, axis=1)
    extent = log_decay.shape[1]
    lower = (jnp.arange(extent)[:, None] >= jnp.arange(extent)[None, :])[None, :, :, None]
    spread = running[:, :, None, :] - running[:, None, :, :]
    decay = jnp.where(lower, jnp.exp(jnp.where(lower, spread, 0.0)), 0.0)
    intersection = jnp.einsum('sqn,skn->sqk', readout, inject, precision=PRECISE_MODE)
    mixing = decay * intersection[:, :, :, None] * step_size[:, None, :, :]
    outputs = jnp.einsum('sqkh,skhp->sqhp', mixing, values, precision=PRECISE_MODE)
    carried = jnp.einsum('sqn,shpn->sqhp', readout, carry_state, precision=PRECISE_MODE)
    outputs = outputs + carried * jnp.exp(running)[:, :, :, None]
    toward_end = jnp.exp(running[:, -1:, :] - running) * step_size
    gained = jnp.einsum('skh,skhp,skn->shpn', toward_end, values, inject, precision=PRECISE_MODE)
    carry_state = carry_state * jnp.exp(running[:, -1, :])[:, :, None, None] + gained
    return (carry_state, outputs)

def span_pass(values, step_size, log_decay, inject, readout, start):
    batch_seqs = step_size.shape[0]
    length = step_size.shape[1]
    block = min(BLOCK_LEN, length)
    count = length // block

    def split(array):
        shaped = array.reshape((batch_seqs, count, block) + array.shape[2:])
        return jnp.moveaxis(shaped, 1, 0)
    final, outputs = lax.scan(jax.checkpoint(block_step), start, (split(values), split(step_size), split(log_decay), split(inject), split(readout)))
    outputs = jnp.moveaxis(outputs, 0, 1).reshape(values.shape)
    return (outputs, final)

def forward(input_row, input_gain, main_in_weight, weight_shared, step_in_weight, filter_main, filter_shared, head_terms, output_gain, out_projection_weight):
    length = input_row.shape[1]
    scale_in = lax.rsqrt(lax.optimization_barrier(jnp.mean(input_row * input_row, axis=-1, keepdims=True)) + EPSILON)
    reduced_output = reduced_width(input_row * scale_in * input_gain)
    gate_before_act = reduced_width_back(jnp.einsum('zni,iw->znw', reduced_output, main_in_weight[:, 0, :], precision=PRECISE_MODE))
    merged_rows = jnp.concatenate([main_in_weight[:, 1, :], weight_shared], axis=1)
    mixer_input = reduced_width_back(reduced_width(jnp.einsum('zni,iw->znw', reduced_output, merged_rows, precision=PRECISE_MODE)))
    step_before_act = reduced_width_back(jnp.einsum('yjz,zq->yjq', reduced_output, step_in_weight, precision=PRECISE_MODE))
    taps = jnp.concatenate([filter_main, filter_shared], axis=1)
    reach = CONV - 1
    padded = jnp.pad(mixer_input, ((0, 0), (reach, 0), (0, 0)))
    conv_pre = taps[CONV]
    for offset in range(CONV):
        conv_pre = conv_pre + taps[offset] * padded[:, offset:offset + length, :]
    active = jax.nn.silu(conv_pre)
    values = active[:, :, :INNER].reshape(1, length, HEADS, HEADDIM)
    inject = active[:, :, INNER:INNER + STATE]
    readout = active[:, :, INNER + STATE:]
    step_size = jax.nn.softplus(step_before_act + head_terms[0])
    log_decay = step_size * -jnp.exp(head_terms[1])
    start = jnp.zeros((1, HEADS, HEADDIM, STATE), jnp.float32)
    scanned, final_state = span_pass(values, step_size, log_decay, inject, readout, start)
    scanned = scanned + head_terms[2][:, None] * values
    gated = scanned.reshape(1, length, INNER) * jax.nn.silu(gate_before_act)
    scale_out = lax.rsqrt(lax.optimization_barrier(jnp.mean(gated * gated, axis=-1, keepdims=True)) + EPSILON)
    normalized_output = reduced_width(gated * scale_out * output_gain)
    return input_row + jnp.einsum('aqn,nf->aqf', normalized_output, out_projection_weight, precision=PRECISE_MODE)

def reference(residual_in, lengths, input_gain, main_in_weight, weight_shared, step_in_weight, filter_main, filter_shared, head_terms, output_gain, out_projection_weight, cotangent):
    params = (input_gain, main_in_weight.astype(jnp.float32), weight_shared.astype(jnp.float32), step_in_weight.astype(jnp.float32), filter_main, filter_shared, head_terms, output_gain, out_projection_weight.astype(jnp.float32))
    places = jnp.arange(LEN, dtype=jnp.int32)

    def one_sequence(totals, item):
        x_seq, cot_seq, valid = item
        live = (places < valid).astype(jnp.float32)[:, None]
        input_row = x_seq.astype(jnp.float32)[None]
        result, pullback = jax.vjp(forward, input_row, *params)
        grads = pullback((cot_seq.astype(jnp.float32) * live)[None])
        totals = jax.tree.map(jnp.add, totals, tuple(grads[1:]))
        return (totals, (result[0].astype(jnp.bfloat16), grads[0][0].astype(jnp.bfloat16)))
    zeros = jax.tree.map(jnp.zeros_like, params)
    totals, (block_out, input_grad) = lax.scan(one_sequence, zeros, (residual_in, cotangent, lengths))
    return (block_out, input_grad, totals[0], totals[1], totals[2], totals[3], totals[4], totals[5], totals[6], totals[7], totals[8])
```

```python
import functools

import jax
import jax.numpy as jnp
from jax import lax
from jax.experimental import pallas as pl
from jax.experimental.pallas import tpu as pltpu
from jax.sharding import PartitionSpec as P

HEADDIM = 64
CONV = 4
BLOCK_LEN = 256
EPSILON = 1e-05
LOG2E = 1.4426950408889634
LANES = 128
SEG = 16
HALO = 16
VMEM = 60 * 1024 * 1024
STREAMS = 2

F32 = jnp.float32
LOW = jnp.bfloat16


def shifted(block, axis, distance):
    devices = range(lax.axis_size(axis))
    route = [(i - distance, i) for i in devices if i - distance in devices]
    return lax.ppermute(block, axis, route)


def mm(a, b):
    return lax.dot_general(a, b, (((1,), (0,)), ((), ())), preferred_element_type=F32)


def mm_nt(a, b):
    return lax.dot_general(a, b, (((1,), (1,)), ((), ())), preferred_element_type=F32)


def mm_tn(a, b):
    return lax.dot_general(a, b, (((0,), (0,)), ((), ())), preferred_element_type=F32)


def halves(a):
    high = a.astype(LOW)
    return high, (a - high.astype(F32)).astype(LOW)


def sigmoid(v):
    return 0.5 * jnp.tanh(0.5 * v) + 0.5


def lane_of(shape):
    return lax.broadcasted_iota(jnp.int32, shape, 1)


def first_lanes(a, count):
    return jnp.where(lane_of(a.shape) < count, a, 0.0)


def pieces_of(a):
    high = a.astype(LOW).astype(F32)
    rest = a - high
    middle = rest.astype(LOW).astype(F32)
    least = rest - middle
    return (high + pltpu.roll(middle, SEG, 1) + pltpu.roll(least, 2 * SEG, 1)).astype(LOW)


def spread_heads(a, one_hot):
    return mm(pieces_of(a), one_hot)


def sum_heads(a, one_hot_t):
    high, least = halves(a)
    return mm(high, one_hot_t) + mm(least, one_hot_t)


def running_sum(a, triangle, heads):
    p = mm(triangle, pieces_of(a))
    p = p + pltpu.roll(p, LANES - SEG, 1) + pltpu.roll(p, LANES - 2 * SEG, 1)
    return first_lanes(p, heads)


def row_sums(a):
    rows, width = a.shape
    return jnp.sum(a.reshape(rows // 8, 8, width), axis=0)


def lower(extent):
    return lax.broadcasted_iota(jnp.int32, (extent, extent), 0) >= lane_of((extent, extent))


def pair_split(tile):
    first = lane_of(tile.shape) < HEADDIM
    zero = jnp.zeros_like(tile)
    return jnp.where(first, tile, zero), jnp.where(first, zero, tile)


def params(vmem=VMEM):
    return pltpu.CompilerParams(dimension_semantics=("arbitrary",), vmem_limit_bytes=vmem)


def whole(shape):
    return pl.BlockSpec(shape, lambda i: (0,) * len(shape), pipeline_mode=pl.Buffered(1))


def per_seq(*shape, offset=0):
    return pl.BlockSpec((1,) + shape, lambda i: (i + offset,) + (0,) * len(shape))


def project_kernel(
    heads, width, state, block,
    x_ref, halo_ref, gain_ref, main_w, side_w, taps_ref, terms_ref, hot_ref,
    low_ref, mixed_ref, edge_ref, pre_ref, gate_ref, heads_ref, step_ref, y_ref, state_ref, end_ref, through_ref,
    low_scr, mix_scr, k_scr,
):
    rows = x_ref.shape[1]
    gain = gain_ref[...]

    def lowered(x):
        x = x.astype(F32)
        scale = lax.rsqrt(jnp.mean(x * x, axis=1, keepdims=True) + EPSILON)
        return (x * scale * gain).astype(LOW)

    low_scr[:HALO] = lowered(halo_ref[0])
    low_scr[HALO:] = lowered(x_ref[0])
    low_ref[0] = low_scr[HALO:]
    gate_ref[0] = mm(low_scr[HALO:], main_w[:, :width])
    main_in = mm(low_scr[...], main_w[:, width:]).astype(LOW)
    side_in = mm(low_scr[...], side_w[...])
    mix_scr[:, :width] = main_in.astype(F32)
    mix_scr[:, width:] = side_in[:, : 2 * state].astype(LOW).astype(F32)
    mixed_ref[0] = mix_scr[HALO:].astype(LOW)
    edge_ref[0] = mix_scr[:HALO].astype(LOW)
    conv = taps_ref[CONV : CONV + 1]
    for k in range(CONV):
        at = HALO - (CONV - 1) + k
        conv = conv + taps_ref[k : k + 1] * mix_scr[at : at + rows]
    pre_ref[0] = conv
    active = conv * sigmoid(conv)
    step_arg = side_in[HALO:, 2 * state :] + terms_ref[0:1]
    step = jnp.maximum(step_arg, 0.0) + jnp.log1p(jnp.exp(-jnp.abs(step_arg)))
    step = first_lanes(step, heads)
    slope = first_lanes(sigmoid(step_arg), heads)
    decay2 = step * (terms_ref[1:2] * LOG2E)
    hot = hot_ref[...]
    triangle = lower(block).astype(F32).astype(LOW)
    sub = block // 2
    tri_sub = lower(sub)
    k_scr[:, :sub, sub:block] = jnp.zeros((2, sub, sub), LOW)
    k_scr[:, :sub, block + sub :] = jnp.zeros((2, sub, sub), LOW)
    held = None
    for b in range(rows // block):
        span = slice(b * block, (b + 1) * block)
        run = running_sum(decay2[span], triangle, heads)
        heads_ref[0, span] = step[span] + pltpu.roll(run, SEG, 1) + pltpu.roll(slope[span], 2 * SEG, 1)
        last = run[block - 1 : block]
        toward = jnp.exp2(last - run)
        values = active[span, :width]
        stepped = spread_heads(step[span], hot) * values
        step_low = stepped.astype(LOW)
        step_ref[0, span] = step_low
        inject_h, inject_l = halves(active[span, width : width + state])
        readout_h, readout_l = halves(active[span, width + state :])
        meet = mm_nt(readout_h, inject_h) + mm_nt(readout_l, inject_h) + mm_nt(readout_h, inject_l)
        meet_tiles = {
            (0, 0): jnp.where(tri_sub, meet[:sub, :sub], 0.0),
            (1, 0): meet[sub:, :sub],
            (1, 1): jnp.where(tri_sub, meet[sub:, sub:], 0.0),
        }
        run_t = jnp.transpose(run)
        for pair in range(heads // 2):
            slot = pair % 2
            for j in range(2):
                h = 2 * pair + j
                for (r, c), tile in meet_tiles.items():
                    gap = run[r * sub : (r + 1) * sub, h : h + 1] - run_t[h : h + 1, c * sub : (c + 1) * sub]
                    at = j * block + c * sub
                    k_scr[slot, r * sub : (r + 1) * sub, at : at + sub] = (
                        tile * jnp.exp2(jnp.minimum(gap, 0.0))
                    ).astype(LOW)
            lanes = slice(pair * LANES, (pair + 1) * LANES)
            one, two = pair_split(step_low[:, lanes])
            y_ref[0, span, lanes] = mm(k_scr[slot], jnp.concatenate([one, two], axis=0))
        weighed = (spread_heads(first_lanes(toward, heads), hot) * stepped).astype(LOW)
        gained = mm_tn(inject_h, weighed)
        through = spread_heads(first_lanes(jnp.broadcast_to(jnp.exp2(last), (8, LANES)), heads), hot)
        if held is not None:
            gained = gained + held * through[0:1]
            total_through = total_through * through
        else:
            total_through = through
        held = gained
        state_ref[0, b] = held
    end_ref[0] = held
    through_ref[0] = total_through


def gate_kernel(
    heads, width, state, block,
    y_in, pre_ref, gate_ref, heads_ref, state_ref, back_ref, gain_ref, skip_ref, hot_ref, *refs,
):
    y_ref, enter_ref, stats_ref = refs[-3:]
    rows = y_in.shape[1]
    hot = hot_ref[...]
    enter = decayed = sum(ref[0] for ref in refs[:-3])
    enter_ref[0] = enter
    gain = gain_ref[...]
    skip = skip_ref[...]
    for b in range(rows // block):
        span = slice(b * block, (b + 1) * block)
        run = first_lanes(pltpu.roll(heads_ref[0, span], LANES - SEG, 1), heads)
        grown = spread_heads(first_lanes(jnp.exp2(run), heads), hot)
        pre = pre_ref[0, span]
        active = pre * sigmoid(pre)
        readout_h, readout_l = halves(active[:, width + state :])
        enter_h, enter_l = halves(enter)
        carried = mm(readout_h, enter_h) + mm(readout_l, enter_h) + mm(readout_h, enter_l)
        y = y_in[0, span] + grown * carried
        y_ref[0, span] = y
        decayed = decayed * grown[block - 1 : block]
        enter = state_ref[0, b] + decayed
        scanned = y + skip * active[:, :width]
        gate = gate_ref[0, span]
        gated = scanned * (gate * sigmoid(gate))
        squares = jnp.sum(gated * gated, axis=1, keepdims=True)
        inner = jnp.sum(gated * (back_ref[0, span] * gain), axis=1, keepdims=True)
        lane = lane_of((block, LANES))
        stats = jnp.where(lane == 0, squares, jnp.where(lane == 1, inner, 0.0))
        stats_ref[0, :, span] = jnp.transpose(stats)[:8]


def out_kernel(
    heads, width, state, block, inner_total, rank_ref,
    y_ref, pre_ref, gate_ref, heads_ref, back_ref, stats_ref, gain_ref, skip_ref, hot_ref,
    normed_ref, grad_y_ref, grad_gate_ref, adjoint_ref, sums_ref, *out_refs,
):
    rows = y_ref.shape[1]

    @pl.when(pl.program_id(0) == 0)
    def _():
        sums_ref[...] = jnp.zeros_like(sums_ref)

    hot = hot_ref[...]
    gain = gain_ref[...]
    skip = skip_ref[...]
    held = None
    for b in reversed(range(rows // block)):
        span = slice(b * block, (b + 1) * block)
        total = jnp.sum(stats_ref[:, 0, :, span], axis=0)
        total = jnp.transpose(jnp.concatenate([total, jnp.zeros((LANES - 8, block), F32)], axis=0))
        scale = lax.rsqrt(total[:, 0:1] / inner_total + EPSILON)
        bend = scale * scale * scale * (total[:, 1:2] / inner_total)
        pre = pre_ref[0, span]
        active = pre * sigmoid(pre)
        values = active[:, :width]
        scanned = y_ref[0, span] + skip * values
        gate = gate_ref[0, span]
        sig = sigmoid(gate)
        gate_act = gate * sig
        gated = scanned * gate_act
        normed = (gated * scale * gain).astype(LOW)
        normed_ref[0, span] = normed
        back = back_ref[0, span]
        grad_gated = scale * (back * gain) - gated * bend
        grad_y = grad_gated * gate_act
        grad_y_ref[0, span] = grad_y
        grad_gate_ref[0, span] = (grad_gated * scanned * (sig * (1.0 + gate * (1.0 - sig)))).astype(LOW)
        sums_ref[:8] += row_sums(back * gated * scale)
        sums_ref[8:] += row_sums(grad_y * values)
        run = first_lanes(pltpu.roll(heads_ref[0, span], LANES - SEG, 1), heads)
        grown = spread_heads(first_lanes(jnp.exp2(run), heads), hot)
        gained = mm_tn(active[:, width + state :].astype(LOW), (grown * grad_y).astype(LOW))
        if held is not None:
            gained = gained + held * grown[block - 1 : block]
        held = gained
        adjoint_ref[0, b] = held
    by_rank(normed_ref[0], rank_ref[0], out_refs)


def back_kernel(
    heads, width, state, block,
    y_ref, pre_ref, mixed_ref, edge_ref, heads_ref, step_ref, grad_y_ref, enter_ref, state_ref, adjoint_ref,
    taps_ref, terms_ref, skip_ref, hot_ref, hot_t_ref, *refs,
):
    leave_refs, refs = refs[:-10], refs[-10:]
    (
    grad_mixed_ref, grad_step_ref, head_ref, tail_ref, filter_ref, terms_out_ref,
    k_scr, u_scr, cross_scr, conv_scr,
    ) = refs
    rows = y_ref.shape[1]
    blocks = rows // block

    @pl.when(pl.program_id(0) == 0)
    def _():
        filter_ref[...] = jnp.zeros_like(filter_ref)
        terms_out_ref[...] = jnp.zeros_like(terms_out_ref)

    hot = hot_ref[...]
    hot_t = hot_t_ref[...]
    skip = skip_ref[...]
    sub = block // 2
    tri = lower(block)
    upper_sub = jnp.logical_not(lower(sub)) | (
        lax.broadcasted_iota(jnp.int32, (sub, sub), 0) == lane_of((sub, sub))
    )
    upper = jnp.logical_not(tri) | (
        lax.broadcasted_iota(jnp.int32, (block, block), 0) == lane_of((block, block))
    )
    suffix = upper.astype(F32).astype(LOW)
    rate = terms_ref[1:2]
    k_scr[:, sub:, :sub] = jnp.zeros((2, sub, sub), LOW)
    k_scr[:, sub:, block : block + sub] = jnp.zeros((2, sub, sub), LOW)
    conv_scr[:HALO] = jnp.zeros((HALO, conv_scr.shape[1]), F32)
    conv_scr[HALO + rows :] = jnp.zeros((HALO, conv_scr.shape[1]), F32)
    leave = sum(ref[0].astype(F32) for ref in leave_refs)
    runs = [first_lanes(pltpu.roll(heads_ref[0, b * block : (b + 1) * block], LANES - SEG, 1), heads) for b in range(blocks)]
    enters = [enter_ref[0]]
    decayed = enter_ref[0]
    for b in range(blocks):
        last = jnp.broadcast_to(jnp.exp2(runs[b][block - 1 : block]), (8, LANES))
        decayed = decayed * spread_heads(first_lanes(last, heads), hot)[0:1]
        enters.append(state_ref[0, b] + decayed)
    for b in reversed(range(blocks)):
        span = slice(b * block, (b + 1) * block)
        packed = heads_ref[0, span]
        step = first_lanes(packed, heads)
        slope_step = first_lanes(pltpu.roll(packed, LANES - 2 * SEG, 1), heads)
        run = runs[b]
        last = run[block - 1 : block]
        pre = pre_ref[0, span]
        sig = sigmoid(pre)
        active = pre * sig
        slope = sig * (1.0 + pre * (1.0 - sig))
        values = active[:, :width]
        inject_h, inject_l = halves(active[:, width : width + state])
        readout_h, readout_l = halves(active[:, width + state :])
        step_low = step_ref[0, span]
        grad_y = grad_y_ref[0, span]
        grad_low = grad_y.astype(LOW)
        leave_low = leave.astype(LOW)
        toward = spread_heads(first_lanes(jnp.exp2(last - run), heads), hot)
        grown = spread_heads(first_lanes(jnp.exp2(run), heads), hot)
        grown_h, grown_l = halves(grown * grad_y)
        u_scr[...] = toward * mm(inject_h, leave_low)
        meet = mm_nt(inject_h, readout_h) + mm_nt(inject_h, readout_l) + mm_nt(inject_l, readout_h)
        meet_tiles = {
            (0, 0): jnp.where(upper_sub, meet[:sub, :sub], 0.0),
            (0, 1): meet[:sub, sub:],
            (1, 1): jnp.where(upper_sub, meet[sub:, sub:], 0.0),
        }
        run_t = jnp.transpose(run)
        cross_scr[...] = jnp.zeros_like(cross_scr)
        for pair in range(heads // 2):
            slot = pair % 2
            lanes = slice(pair * LANES, (pair + 1) * LANES)
            tile_low = step_low[:, lanes]
            split = pair_split(grad_low[:, lanes])
            for j in range(2):
                h = 2 * pair + j
                products = {}
                top = mm_nt(tile_low[:sub], split[j])
                products[(0, 0)] = top[:, :sub]
                products[(0, 1)] = top[:, sub:]
                products[(1, 1)] = mm_nt(tile_low[sub:], split[j][sub:])
                for (r, c), tile in meet_tiles.items():
                    gap = run_t[h : h + 1, c * sub : (c + 1) * sub] - run[r * sub : (r + 1) * sub, h : h + 1]
                    fall = jnp.exp2(jnp.minimum(gap, 0.0))
                    at = j * block + c * sub
                    k_scr[slot, r * sub : (r + 1) * sub, at : at + sub] = (tile * fall).astype(LOW)
                    cross_scr[r * sub : (r + 1) * sub, c * sub : (c + 1) * sub] += fall * products[(r, c)]
            u_scr[:, lanes] += mm(k_scr[slot], jnp.concatenate(split, axis=0))
        cross = jnp.where(upper, cross_scr[...], 0.0).astype(LOW)
        enter_h, enter_l = halves(enters[b])
        grad_readout = (
            mm_tn(cross, inject_h) + mm_nt(grown_h, enter_h) + mm_nt(grown_l, enter_h) + mm_nt(grown_h, enter_l)
        )
        weighed = (toward * step_low.astype(F32)).astype(LOW)
        grad_inject = mm(cross, readout_h) + mm_nt(weighed, leave_low)
        u = u_scr[...]
        grad_step = sum_heads(values * u, hot_t)
        taken = step_low.astype(F32) * u
        given = grad_low.astype(F32) * y_ref[0, span]
        flow = running_sum(sum_heads(given - taken, hot_t), suffix, heads)
        ends = jnp.sum(leave * enters[b + 1], axis=0, keepdims=True)
        flow = flow + first_lanes(sum_heads(jnp.broadcast_to(ends, (8, width)), hot_t)[0:1], heads)
        grad_arg = (grad_step + rate * flow) * slope_step
        grad_step_ref[0, span] = grad_arg.astype(LOW)
        terms_out_ref[:8] += row_sums(grad_arg)
        terms_out_ref[8:] += row_sums(flow * step * rate)
        grad_values = spread_heads(step, hot) * u + skip * grad_y
        conv_scr[HALO + b * block : HALO + (b + 1) * block, :width] = grad_values * slope[:, :width]
        conv_scr[HALO + b * block : HALO + (b + 1) * block, width : width + state] = (
            grad_inject * slope[:, width : width + state]
        )
        conv_scr[HALO + b * block : HALO + (b + 1) * block, width + state :] = (
            grad_readout * slope[:, width + state :]
        )
        if b:
            leave = adjoint_ref[0, b] + grown[block - 1 : block] * leave
    head_ref[0] = conv_scr[HALO : HALO + 8]
    mixed = mixed_ref[0].astype(F32)
    edge = edge_ref[0].astype(F32)
    total = None
    for k in range(CONV):
        ahead = CONV - 1 - k
        moved = conv_scr[HALO + ahead : HALO + ahead + rows]
        term = taps_ref[k : k + 1] * moved
        total = term if total is None else total + term
        filter_ref[8 * k : 8 * k + 8] += row_sums(mixed * moved) + row_sums(edge * conv_scr[ahead : ahead + HALO])
    filter_ref[8 * CONV :] += row_sums(conv_scr[HALO : HALO + rows])
    high, least = halves(total)
    grad_mixed_ref[0, :, : width + 2 * state] = high
    grad_mixed_ref[0, :, width + 2 * state :] = least[:, width:]
    tail_ref[0] = total[rows - HALO :]


def top_kernel(rows, first, length_ref, place_ref, cot_ref, out_w, top_ref, back_ref):
    valid = length_ref[first + pl.program_id(0)] - place_ref[0]
    cot = cot_ref[0]
    row = lax.broadcasted_iota(jnp.int32, cot.shape, 0)
    top = jnp.where(row < valid, cot.astype(F32), 0.0).astype(LOW)
    top_ref[0] = top
    back_ref[0] = mm_nt(top, out_w[...])


def by_rank(rows, rank, out_refs):
    share = out_refs[0].shape[0]
    count = rows.shape[0] // share
    for k in range(count):
        place = (pl.program_id(0) * count + k) ^ rank
        for d in range(len(out_refs)):

            @pl.when(place == d)
            def _(k=k, d=d):
                out_refs[d][...] = rows[k * share : (k + 1) * share]


def lowered_kernel(width, state, gate_ref, mixed_ref, step_ref, main_w, side_w, out_ref):
    main = jnp.concatenate([gate_ref[0], mixed_ref[0, :, :width]], axis=1)
    side = jnp.concatenate([mixed_ref[0, :, width : width + 2 * state], step_ref[0]], axis=1)
    out_ref[0] = (mm_nt(main, main_w[...]) + mm_nt(side, side_w[...])).astype(LOW)


def product_kernel(ranks, rank_ref, *refs):
    x_refs, weight_ref = refs[:STREAMS], refs[STREAMS]
    parts = refs[STREAMS + 1 : -2]
    out_ref, acc_ref = refs[-2:]
    share = parts[0].shape[0]
    at = pl.program_id(0)
    for d in range(ranks):

        @pl.when(at == d)
        def _(d=d):
            rows = jnp.concatenate([parts[s * ranks + d][...] for s in range(STREAMS)], axis=0)
            part = mm(rows, weight_ref[0])
            if d == 0:
                part = part + jnp.concatenate([x[0].astype(F32) for x in x_refs], axis=0)
            else:
                part = part + acc_ref[...]
            acc_ref[...] = part

    @pl.when(at == ranks - 1)
    def _():
        for s in range(STREAMS):
            out_ref[s] = acc_ref[s * share : (s + 1) * share].astype(LOW)


def merged(ref):
    return ref[...].reshape(ref.shape[0] * ref.shape[1], ref.shape[2])


def lane_sums(a):
    return sum(a[:, k : k + LANES] for k in range(0, a.shape[1], LANES))


def gate_grad_kernel(*refs):
    low, grads = refs[:STREAMS], refs[STREAMS : 2 * STREAMS]
    main_w, out_ref, gain_ref = refs[2 * STREAMS :]
    gate = sum(mm_tn(merged(a), merged(b)) for a, b in zip(low, grads))
    out_ref[...] = gate.astype(LOW)
    gain_ref[...] = lane_sums(main_w[...].astype(F32) * gate)


def out_grad_kernel(*refs):
    top, normed, out_ref = refs[:STREAMS], refs[STREAMS : 2 * STREAMS], refs[-1]
    out_ref[...] = sum(mm_tn(merged(a), merged(b)) for a, b in zip(top, normed)).astype(LOW)


def late_kernel(width, state, *refs):
    low, mixed, step = (refs[k * STREAMS : (k + 1) * STREAMS] for k in range(3))
    main_w, side_w, gain_in, own_ref, shared_ref, gain_ref = refs[3 * STREAMS :]
    total = sum(mm_tn(merged(a), merged(b)) for a, b in zip(low, mixed))
    steps = sum(mm_tn(merged(a), merged(b)) for a, b in zip(low, step))
    main = total[:, :width]
    shared = total[:, width : width + 2 * state] + total[:, width + 2 * state :]
    own_ref[:, :width] = main.astype(LOW)
    own_ref[:, width:] = steps.astype(LOW)
    shared_ref[...] = shared
    side = side_w[...].astype(F32)
    gain_ref[...] = (
        gain_in[...]
        + lane_sums(main_w[...].astype(F32) * main)
        + lane_sums(side[:, : 2 * state] * shared)
        + side[:, 2 * state :] * steps
    )


def by_rank(rows, rank, out_refs):
    share = out_refs[0].shape[0]
    count = rows.shape[0] // share
    for k in range(count):
        place = (pl.program_id(0) * count + k) ^ rank
        for d in range(len(out_refs)):

            @pl.when(place == d)
            def _(k=k, d=d):
                out_refs[d][...] = rows[k * share : (k + 1) * share]


def lowered_kernel(width, state, rank_ref, gate_ref, mixed_ref, step_ref, main_w, side_w, *out_refs):
    main = jnp.concatenate([gate_ref[0], mixed_ref[0, :, :width]], axis=1)
    side = jnp.concatenate([mixed_ref[0, :, width : width + 2 * state], step_ref[0]], axis=1)
    total = (mm_nt(main, main_w[...]) + mm_nt(side, side_w[...])).astype(LOW)
    by_rank(total, rank_ref[0], out_refs)


def norm_kernel(ranks, rank_ref, x_ref, top_ref, gain_ref, *refs):
    out_ref = refs[ranks]
    x = x_ref[0].astype(F32)
    scale = lax.rsqrt(jnp.mean(x * x, axis=1, keepdims=True) + EPSILON)
    normed = x * scale
    grad = sum(ref[...].astype(F32) for ref in refs[:ranks])
    scaled = grad * gain_ref[...]
    out = top_ref[0].astype(F32) + scale * (scaled - normed * jnp.mean(scaled * normed, axis=1, keepdims=True))
    out_ref[...] = out.astype(LOW)


def per_device(
    residual_in,
    lengths,
    input_gain,
    main_in_weight,
    weight_shared,
    step_in_weight,
    filter_main,
    filter_shared,
    head_terms,
    output_gain,
    out_projection_weight,
    cotangent,
):
    all_seqs, rows, model = residual_in.shape
    seqs = all_seqs // STREAMS
    heads = step_in_weight.shape[1]
    width = main_in_weight.shape[2]
    state = weight_shared.shape[1] // 2
    mixed_width = width + 2 * state
    kept_width = mixed_width + 2 * state
    ranks = lax.axis_size("tensor")
    spans = lax.axis_size("seq")
    inner_total = width * ranks
    reach = CONV - 1
    block = min(BLOCK_LEN, rows)
    blocks = rows // block
    share = seqs * rows // ranks
    sds = jax.ShapeDtypeStruct

    main_w = main_in_weight.reshape(model, 2 * width)
    side_w = jnp.concatenate(
        [weight_shared, jnp.pad(step_in_weight, ((0, 0), (0, LANES - heads)))], axis=1
    )
    side_width = side_w.shape[1]
    taps = jnp.pad(jnp.concatenate([filter_main, filter_shared], axis=1), ((0, 8 - CONV - 1), (0, 0)))
    rate = -jnp.exp(head_terms[1])
    terms = jnp.pad(jnp.stack([head_terms[0], rate]), ((0, 6), (0, LANES - heads)))
    skip = jnp.repeat(head_terms[2], HEADDIM)[None]
    channel_head = jnp.arange(width, dtype=jnp.int32)[None, :] // HEADDIM
    lane = jnp.arange(LANES, dtype=jnp.int32)[:, None]
    hot = ((lane % SEG == channel_head) & (lane < 3 * SEG)).astype(LOW)
    hot_t = (lane == channel_head).astype(LOW).T
    in_gain = input_gain[None]
    out_gain = output_gain[None]
    dims = (heads, width, state, block)
    place = (lax.axis_index("seq") * rows).astype(jnp.int32)[None]
    rank = lax.axis_index("tensor").astype(jnp.int32)[None]
    halo = shifted(residual_in[:, rows - HALO :, :], "seq", 1)
    full_w = lax.all_gather(out_projection_weight, "tensor", axis=0)
    smem = pl.BlockSpec(memory_space=pltpu.SMEM)

    def cost(flops):
        return pl.CostEstimate(flops=int(flops), bytes_accessed=30 << 20, transcendentals=0)

    def after(value, *others):
        return lax.optimization_barrier((value,) + others)[0]

    def project(s, halo):
        return pl.pallas_call(
            functools.partial(project_kernel, *dims),
            grid=(seqs,),
            in_specs=[
                per_seq(rows, model, offset=s * seqs), per_seq(HALO, model, offset=s * seqs), whole((1, model)),
                whole((model, 2 * width)), whole((model, side_width)), whole((8, mixed_width)), whole((8, LANES)),
                whole((LANES, width)),
            ],
            out_specs=[
                per_seq(rows, model), per_seq(rows, mixed_width), per_seq(HALO, mixed_width),
                per_seq(rows, mixed_width), per_seq(rows, width), per_seq(rows, LANES), per_seq(rows, width),
                per_seq(rows, width), per_seq(blocks, state, width), per_seq(state, width), per_seq(8, width),
            ],
            out_shape=[
                sds((seqs, rows, model), LOW), sds((seqs, rows, mixed_width), LOW),
                sds((seqs, HALO, mixed_width), LOW), sds((seqs, rows, mixed_width), F32),
                sds((seqs, rows, width), F32), sds((seqs, rows, LANES), F32), sds((seqs, rows, width), LOW),
                sds((seqs, rows, width), F32), sds((seqs, blocks, state, width), F32),
                sds((seqs, state, width), F32), sds((seqs, 8, width), F32),
            ],
            scratch_shapes=[
                pltpu.VMEM((HALO + rows, model), LOW), pltpu.VMEM((HALO + rows, mixed_width), F32),
                pltpu.VMEM((2, block, 2 * block), LOW),
            ],
            compiler_params=params(),
            cost_estimate=cost(8e9 * seqs),
            name="project",
        )(residual_in, halo, in_gain, main_w, side_w, taps, terms, hot)

    def chained(local, through, direction, kind, marks):
        arrivals = []
        for hop in range(spans - 1):
            sender = hop if direction > 0 else spans - 1 - hop
            sent = local if hop == 0 else local + through[:, :1] * arrivals[-1].astype(F32)
            arrived = lax.ppermute(sent.astype(kind), "seq", [(sender, sender + direction)])
            arrivals.append(after(arrived, marks[min(hop, len(marks) - 1)]))
        return arrivals

    def top_of(s, place):
        return pl.pallas_call(
            functools.partial(top_kernel, rows, s * seqs),
            grid=(seqs,),
            in_specs=[smem, smem, per_seq(rows, model, offset=s * seqs), whole((width, model))],
            out_specs=[per_seq(rows, model), per_seq(rows, width)],
            out_shape=[sds((seqs, rows, model), LOW), sds((seqs, rows, width), F32)],
            compiler_params=params(),
            cost_estimate=cost(2.5e9 * seqs),
            name="top",
        )(lengths, place, cotangent, out_projection_weight)

    def gated_of(y_local, pre, gate, packed, arrivals, states, back):
        return pl.pallas_call(
            functools.partial(gate_kernel, *dims),
            grid=(seqs,),
            in_specs=[
                per_seq(rows, width), per_seq(rows, mixed_width), per_seq(rows, width), per_seq(rows, LANES),
                per_seq(blocks, state, width), per_seq(rows, width), whole((1, width)),
                whole((1, width)), whole((LANES, width)),
            ]
            + [per_seq(state, width)] * len(arrivals),
            out_specs=[per_seq(rows, width), per_seq(state, width), per_seq(8, rows)],
            out_shape=[sds((seqs, rows, width), F32), sds((seqs, state, width), F32), sds((seqs, 8, rows), F32)],
            compiler_params=params(),
            cost_estimate=cost(4e9 * seqs),
            name="gated",
        )(y_local, pre, gate, packed, states, back, out_gain, skip, hot, *arrivals)

    def outward(y, pre, gate, packed, back, all_stats):
        seq = lambda *shape: pl.BlockSpec((1,) + shape, lambda i, r: (i,) + (0,) * len(shape))
        fixed = lambda *shape: pl.BlockSpec(shape, lambda i, r: (0,) * len(shape))
        return pl.pallas_call(
            functools.partial(out_kernel, *dims, inner_total),
            grid_spec=pltpu.PrefetchScalarGridSpec(
                num_scalar_prefetch=1,
                grid=(seqs,),
                in_specs=[
                    seq(rows, width), seq(rows, mixed_width), seq(rows, width), seq(rows, LANES), seq(rows, width),
                    pl.BlockSpec((ranks, 1, 8, rows), lambda i, r: (0, i, 0, 0)), fixed(1, width), fixed(1, width),
                    fixed(LANES, width),
                ],
                out_specs=[
                    seq(rows, width), seq(rows, width), seq(rows, width), seq(blocks, state, width), fixed(16, width),
                ]
                + [fixed(share, width)] * ranks,
            ),
            out_shape=[
                sds((seqs, rows, width), LOW), sds((seqs, rows, width), F32), sds((seqs, rows, width), LOW),
                sds((seqs, blocks, state, width), F32), sds((16, width), F32),
            ]
            + [sds((share, width), LOW)] * ranks,
            compiler_params=params(),
            cost_estimate=cost(5e9 * seqs),
            name="outward",
        )(rank, y, pre, gate, packed, back, all_stats, out_gain, skip, hot)

    def backward(y, pre, mixed, edge, packed, stepped, grad_y, entering, states, leaving, adjoint):
        return pl.pallas_call(
            functools.partial(back_kernel, *dims),
            grid=(seqs,),
            in_specs=[
                per_seq(rows, width), per_seq(rows, mixed_width), per_seq(rows, mixed_width),
                per_seq(HALO, mixed_width), per_seq(rows, LANES), per_seq(rows, width), per_seq(rows, width),
                per_seq(state, width), per_seq(blocks, state, width),
                per_seq(blocks, state, width), whole((8, mixed_width)), whole((8, LANES)), whole((1, width)),
                whole((LANES, width)), whole((width, LANES)),
            ]
            + [per_seq(state, width)] * len(leaving),
            out_specs=[
                per_seq(rows, kept_width), per_seq(rows, LANES), per_seq(8, mixed_width), per_seq(HALO, mixed_width),
                pl.BlockSpec((8 * (CONV + 1), mixed_width), lambda i: (0, 0)),
                pl.BlockSpec((16, LANES), lambda i: (0, 0)),
            ],
            out_shape=[
                sds((seqs, rows, kept_width), LOW), sds((seqs, rows, LANES), LOW), sds((seqs, 8, mixed_width), F32),
                sds((seqs, HALO, mixed_width), F32), sds((8 * (CONV + 1), mixed_width), F32), sds((16, LANES), F32),
            ],
            scratch_shapes=[
                pltpu.VMEM((2, block, 2 * block), LOW), pltpu.VMEM((block, width), F32),
                pltpu.VMEM((block, block), F32), pltpu.VMEM((2 * HALO + rows, mixed_width), F32),
            ],
            compiler_params=params(),
            cost_estimate=cost(11e9 * seqs),
            name="backward",
        )(
            y, pre, mixed, edge, packed, stepped, grad_y, entering, states, adjoint,
            taps, terms, skip, hot, hot_t, *leaving,
        )

    def lowered_of(grad_gate, grad_mixed, grad_step):
        seq = lambda *shape: pl.BlockSpec((1,) + shape, lambda i, r: (i,) + (0,) * len(shape))
        fixed = lambda *shape: pl.BlockSpec(shape, lambda i, r: (0,) * len(shape), pipeline_mode=pl.Buffered(1))
        return pl.pallas_call(
            functools.partial(lowered_kernel, width, state),
            grid_spec=pltpu.PrefetchScalarGridSpec(
                num_scalar_prefetch=1,
                grid=(seqs,),
                in_specs=[
                    seq(rows, width), seq(rows, kept_width), seq(rows, LANES), fixed(model, 2 * width),
                    fixed(model, side_width),
                ],
                out_specs=[pl.BlockSpec((share, model), lambda i, r: (0, 0))] * ranks,
            ),
            out_shape=[sds((share, model), LOW)] * ranks,
            compiler_params=params(),
            cost_estimate=cost(4.5e9 * seqs),
            name="lowered",
        )(rank, grad_gate, grad_mixed, grad_step, main_w, side_w)

    def input_norm(s, parts, top):
        return pl.pallas_call(
            functools.partial(norm_kernel, ranks),
            grid_spec=pltpu.PrefetchScalarGridSpec(
                num_scalar_prefetch=1,
                grid=(1,),
                in_specs=[
                    pl.BlockSpec((1, share, model), lambda i, r: (s * ranks + r[0], 0, 0)),
                    pl.BlockSpec((1, share, model), lambda i, r: (r[0], 0, 0)),
                    pl.BlockSpec((1, model), lambda i, r: (0, 0)),
                ]
                + [pl.BlockSpec((share, model), lambda i, r: (0, 0))] * ranks,
                out_specs=pl.BlockSpec((share, model), lambda i, r: (0, 0)),
            ),
            out_shape=sds((share, model), LOW),
            compiler_params=params(),
            name="input_norm",
        )(rank, residual_in.reshape(-1, share, model), top.reshape(-1, share, model), in_gain, *parts)

    def product(parts):
        row_of = lambda s: pl.BlockSpec((1, share, model), lambda i, r: (s * ranks + r[0], 0, 0))
        x = residual_in.reshape(-1, share, model)
        return pl.pallas_call(
            functools.partial(product_kernel, ranks),
            grid_spec=pltpu.PrefetchScalarGridSpec(
                num_scalar_prefetch=1,
                grid=(ranks,),
                in_specs=[row_of(s) for s in range(STREAMS)]
                + [pl.BlockSpec((1, width, model), lambda i, r: (r[0] ^ i, 0, 0))]
                + [pl.BlockSpec((share, width), lambda i, r: (0, 0))] * (STREAMS * ranks),
                out_specs=pl.BlockSpec((STREAMS, share, model), lambda i, r: (0, 0, 0)),
                scratch_shapes=[pltpu.VMEM((STREAMS * share, model), F32)],
            ),
            out_shape=sds((STREAMS, share, model), LOW),
            compiler_params=params(),
            cost_estimate=cost(2.4e9 * all_seqs),
            name="product",
        )(rank, *[x] * STREAMS, full_w, *parts)

    tile = 256
    tiles = model // tile
    column = pl.BlockSpec((seqs, rows, tile), lambda i: (0, 0, i))
    row = lambda n: pl.BlockSpec((tile, n), lambda i: (i, 0))

    def gate_grad(low, grads):
        return pl.pallas_call(
            gate_grad_kernel,
            grid=(tiles,),
            in_specs=[column] * STREAMS + [whole((seqs, rows, width))] * STREAMS + [row(width)],
            out_specs=[row(width), row(LANES)],
            out_shape=[sds((model, width), LOW), sds((model, LANES), F32)],
            compiler_params=params(),
            cost_estimate=cost(2.5e9 * all_seqs),
            name="gate_grad",
        )(*low, *grads, main_w)

    def out_grad(top, normed):
        return pl.pallas_call(
            out_grad_kernel,
            grid=(tiles,),
            in_specs=[column] * STREAMS + [whole((seqs, rows, width))] * STREAMS,
            out_specs=row(width),
            out_shape=sds((model, width), LOW),
            compiler_params=params(),
            cost_estimate=cost(2.5e9 * all_seqs),
            name="out_grad",
        )(*top, *normed)

    def late_of(low, mixed, step, gain):
        return pl.pallas_call(
            functools.partial(late_kernel, width, state),
            grid=(tiles,),
            in_specs=[column] * STREAMS
            + [whole((seqs, rows, kept_width))] * STREAMS
            + [whole((seqs, rows, LANES))] * STREAMS
            + [pl.BlockSpec((tile, width), lambda i: (i, 1)), row(side_width), row(LANES)],
            out_specs=[row(width + LANES), row(2 * state), row(LANES)],
            out_shape=[sds((model, width + LANES), LOW), sds((model, 2 * state), F32), sds((model, LANES), F32)],
            compiler_params=params(),
            cost_estimate=cost(5e9 * all_seqs),
            name="late",
        )(*low, *mixed, *step, main_w, side_w, gain)

    def exchanged(own):
        return [own] + [
            lax.ppermute(own, "tensor", [(i, i ^ d) for i in range(ranks)]) for d in range(1, ranks)
        ]

    def swapped(blocks_of):
        return [
            lax.ppermute(b, "tensor", [(i, i ^ d) for i in range(ranks)]) if d else b for d, b in enumerate(blocks_of)
        ]

    def scattered(whole_rows):
        blocks_of = whole_rows.reshape(ranks, share, -1)
        return swapped([lax.dynamic_index_in_dim(blocks_of, rank[0] ^ d, axis=0, keepdims=False) for d in range(ranks)])

    def assembled(ready, pieces):
        held = ready.reshape(-1, share, model)
        count = held.shape[0]

        def kernel(rank_ref, held_ref, *refs):
            out_ref, sems = refs[ranks:]
            copies = [pltpu.make_async_copy(held_ref, out_ref.at[pl.ds(0, count)], sems.at[ranks])]
            for d in range(ranks):
                copies.append(pltpu.make_async_copy(refs[d], out_ref.at[count + (rank_ref[0] ^ d)], sems.at[d]))
            for copy in copies:
                copy.start()
            for copy in copies:
                copy.wait()

        return pl.pallas_call(
            kernel,
            in_specs=[smem] + [pl.BlockSpec(memory_space=pltpu.VMEM)] * (1 + ranks),
            out_specs=pl.BlockSpec(memory_space=pl.ANY),
            out_shape=sds((count + ranks, share, model), LOW),
            scratch_shapes=[pltpu.SemaphoreType.DMA((ranks + 1,))],
            compiler_params=pltpu.CompilerParams(vmem_limit_bytes=VMEM),
            name="assemble",
        )(rank, held, *pieces).reshape(residual_in.shape)

    flat = lambda a: a.reshape(seqs * rows, a.shape[-1])
    both = range(STREAMS)

    def gate_on(values, *marks):
        return list(lax.optimization_barrier(tuple(values) + marks)[: len(values)])

    def backward_of(s, leaving, mark, fill):
        made, step_low, head, tail, filter_sum, term_sum = backward(
            after(y[s], mark), pre[s], mixed[s], edge[s], packed[s], stepped[s], grad_y[s], entering[s], states[s],
            leaving, adjoint[s],
        )
        raw = step_low
        following = after(shifted(head[:, :reach], "seq", -1), fill(raw))
        fix = jnp.zeros((seqs, reach, mixed_width), F32)
        for k in range(reach):
            fix = fix + jnp.pad(taps[k] * following[:, : reach - k], ((0, 0), (k, 0), (0, 0)))
        tail = tail + jnp.pad(fix, ((0, 0), (HALO - reach, 0), (0, 0)))
        tail_high = tail.astype(LOW)
        tail_least = (tail - lax.optimization_barrier(tail_high).astype(F32)).astype(LOW)[:, :, width:]
        made = lax.dynamic_update_slice(
            made, jnp.concatenate([tail_high, tail_least], axis=2), (0, rows - HALO, 0)
        )
        return made, step_low, filter_sum, term_sum, raw

    reduced = lambda a: lax.psum_scatter(a, ("seq", "dp"), scatter_dimension=0, tiled=True)

    first = [project(0, halo)]
    first.append(project(1, after(halo, first[0][-1])))
    low, mixed, edge, pre, gate, packed, stepped, y_local, states, local, through = zip(*first)
    tops = [top_of(0, after(place, local[1]))]
    tops.append(top_of(1, after(place, tops[0][0])))
    top, back = zip(*tops)

    def gated_of_stream(s, arrivals):
        y, entering, stats = gated_of(y_local[s], pre[s], gate[s], packed[s], arrivals, states[s], back[s])
        return y, entering, stats, lax.all_gather(stats, "tensor", axis=0)

    y, entering, stats, all_stats = [None] * 2, [None] * 2, [None] * 2, [None] * 2
    second = []
    arrivals = chained(local[0], through[0], 1, F32, [local[1], top[0], top[1]])
    y[0], entering[0], stats[0], all_stats[0] = gated_of_stream(0, arrivals)
    second.append(outward(y[0], pre[0], gate[0], packed[0], back[0], all_stats[0]))
    arrivals = chained(local[1], through[1], 1, F32, [top[1], stats[0], second[0][0]])
    y[1], entering[1], stats[1], all_stats[1] = gated_of_stream(1, arrivals)
    parts = gate_on(swapped(second[0][5:]), all_stats[1])
    second.append(outward(after(y[1], *parts), pre[1], gate[1], packed[1], back[1], all_stats[1]))
    normed, grad_y, grad_gate, adjoint, out_sums = list(zip(*second))[:5]
    gate_w, gain_sums = gate_grad(gate_on(low, normed[1]), grad_gate)
    gate_w_sum = reduced(gate_w)
    made_out = product(parts + gate_on(swapped(second[1][5:]), gate_w))
    block_out = lax.all_gather(made_out, "tensor", axis=1, tiled=True)
    leaving = chained(adjoint[0][:, 0], through[0], -1, LOW, [stats[1], normed[1], gate_w])
    early = []

    def out_first(raw):
        early.append(out_grad(gate_on(top, raw), normed))
        return early[0]

    third = [backward_of(0, leaving, made_out, out_first)]
    out_w = reduced(early[0])
    leaving = chained(adjoint[1][:, 0], through[1], -1, LOW, [gate_w, made_out, third[0][4]])
    partial = [lowered_of(grad_gate[0], *third[0][:2])]
    first_own = []

    def norm_first(raw):
        first_own.append(input_norm(0, gate_on(swapped(partial[0]), raw), top[0]))
        return first_own[0]

    third.append(backward_of(1, gate_on(leaving, gate_w_sum), partial[0][0], norm_first))
    first_in = lax.all_gather(first_own[0], "tensor", axis=0, tiled=True)
    grad_mixed, grad_step, filter_sums, term_sums = list(zip(*third))[:4]
    grad_own, grad_side, gain_sums = late_of(low, grad_mixed, grad_step, gain_sums)
    partial.append(lowered_of(after(grad_gate[1], grad_own, block_out, out_w), *third[1][:2]))
    grad_own_w = reduced(grad_own).astype(F32)
    shared_w = reduced(grad_side)
    grad_gate_w = gate_w_sum.astype(F32)
    grad_out_w = out_w.astype(F32).T
    grad_main_w = jnp.stack([grad_gate_w, grad_own_w[:, :width]], axis=1)
    grad_shared_w = jnp.sum(lax.all_gather(shared_w, "tensor", axis=0), axis=0)
    grad_step_w = grad_own_w[:, width : width + heads]
    filters = jnp.sum(sum(filter_sums).reshape(CONV + 1, 8, mixed_width), axis=1)
    term_rows = jnp.sum(sum(term_sums).reshape(2, 8, LANES), axis=1)
    out_rows = jnp.sum(sum(out_sums).reshape(2, 8, width), axis=1)
    grad_skip = jnp.pad(jnp.sum(out_rows[1].reshape(heads, HEADDIM), axis=1), (0, LANES - heads))
    everywhere = (jnp.sum(gain_sums, axis=1) / input_gain, filters[:, width:])
    per_rank = (filters[:, :width], jnp.concatenate([term_rows, grad_skip[None]], axis=0), out_rows[0])
    packed_sums = jnp.concatenate([a.reshape(-1) for a in everywhere + per_rank])
    packed_sums = jnp.sum(lax.all_gather(packed_sums.reshape(-1, LANES), ("seq", "dp"), axis=0), axis=0)
    split = (everywhere[0].size + everywhere[1].size) // LANES
    shared_sums = jnp.sum(lax.all_gather(packed_sums[:split], "tensor", axis=0), axis=0).reshape(-1)
    rank_sums = packed_sums[split:].reshape(-1)
    small_in = shared_sums[:model]
    small_shared = shared_sums[model:].reshape(CONV + 1, 2 * state)
    small_main = rank_sums[: (CONV + 1) * width].reshape(CONV + 1, width)
    small_terms = rank_sums[(CONV + 1) * width : -width].reshape(3, LANES)[:, :heads]
    small_out = rank_sums[-width:]
    own = input_norm(1, gate_on(swapped(partial[1]), shared_sums), top[1])
    pieces = exchanged(own)
    return (
        block_out.reshape(residual_in.shape),
        assembled(first_in, gate_on(pieces, grad_out_w)),
        small_in,
        grad_main_w,
        grad_shared_w,
        grad_step_w,
        small_main,
        small_shared,
        small_terms,
        small_out,
        grad_out_w,
    )


def solution(mesh):
    placed = (
        P("dp", "seq", None),
        P("dp"),
        P(),
        P(None, None, "tensor"),
        P(),
        P(None, "tensor"),
        P(None, "tensor"),
        P(),
        P(None, "tensor"),
        P("tensor"),
        P("tensor", None),
        P("dp", "seq", None),
    )
    return jax.shard_map(
        per_device,
        mesh=mesh,
        in_specs=placed,
        out_specs=(
            P("dp", "seq", None),
            P("dp", "seq", None),
            P(),
            P(("seq", "dp"), None, "tensor"),
            P(("seq", "dp"), None),
            P(("seq", "dp"), "tensor"),
            P(None, "tensor"),
            P(),
            P(None, "tensor"),
            P("tensor"),
            P("tensor", ("seq", "dp")),
        ),
        check_vma=False,
    )
```

```python
import functools

import jax
import jax.numpy as jnp
from jax import lax
from jax.experimental import pallas as pl
from jax.experimental.pallas import tpu as pltpu
from jax.sharding import PartitionSpec as P

HEADDIM = 64
CONV = 4
BLOCK_LEN = 256
EPSILON = 1e-05
LOG2E = 1.4426950408889634
LANES = 128
SEG = 16
HALO = 16
VMEM = 60 * 1024 * 1024
STREAMS = 2

F32 = jnp.float32
LOW = jnp.bfloat16


def shifted(block, axis, distance):
    devices = range(lax.axis_size(axis))
    route = [(i - distance, i) for i in devices if i - distance in devices]
    return lax.ppermute(block, axis, route)


def mm(a, b):
    return lax.dot_general(a, b, (((1,), (0,)), ((), ())), preferred_element_type=F32)


def mm_nt(a, b):
    return lax.dot_general(a, b, (((1,), (1,)), ((), ())), preferred_element_type=F32)


def mm_tn(a, b):
    return lax.dot_general(a, b, (((0,), (0,)), ((), ())), preferred_element_type=F32)


def halves(a):
    high = a.astype(LOW)
    return high, (a - high.astype(F32)).astype(LOW)


def sigmoid(v):
    return 0.5 * jnp.tanh(0.5 * v) + 0.5


def lane_of(shape):
    return lax.broadcasted_iota(jnp.int32, shape, 1)


def first_lanes(a, count):
    return jnp.where(lane_of(a.shape) < count, a, 0.0)


def pieces_of(a):
    high = a.astype(LOW).astype(F32)
    rest = a - high
    middle = rest.astype(LOW).astype(F32)
    least = rest - middle
    return (high + pltpu.roll(middle, SEG, 1) + pltpu.roll(least, 2 * SEG, 1)).astype(LOW)


def spread_heads(a, one_hot):
    return mm(pieces_of(a), one_hot)


def sum_heads(a, one_hot_t):
    high, least = halves(a)
    return mm(high, one_hot_t) + mm(least, one_hot_t)


def running_sum(a, triangle, heads):
    p = mm(triangle, pieces_of(a))
    p = p + pltpu.roll(p, LANES - SEG, 1) + pltpu.roll(p, LANES - 2 * SEG, 1)
    return first_lanes(p, heads)


def row_sums(a):
    rows, width = a.shape
    return jnp.sum(a.reshape(rows // 8, 8, width), axis=0)


def lower(extent):
    return lax.broadcasted_iota(jnp.int32, (extent, extent), 0) >= lane_of((extent, extent))


def pair_split(tile):
    first = lane_of(tile.shape) < HEADDIM
    zero = jnp.zeros_like(tile)
    return jnp.where(first, tile, zero), jnp.where(first, zero, tile)


def params(vmem=VMEM):
    return pltpu.CompilerParams(dimension_semantics=("arbitrary",), vmem_limit_bytes=vmem)


def whole(shape):
    return pl.BlockSpec(shape, lambda i: (0,) * len(shape), pipeline_mode=pl.Buffered(1))


def per_seq(*shape, offset=0):
    return pl.BlockSpec((1,) + shape, lambda i: (i + offset,) + (0,) * len(shape))


def project_kernel(
    heads, width, state, block,
    x_ref, halo_ref, gain_ref, main_w, side_w, taps_ref, terms_ref, hot_ref,
    low_ref, mixed_ref, edge_ref, pre_ref, gate_ref, heads_ref, step_ref, y_ref, state_ref, end_ref, through_ref,
    low_scr, mix_scr, k_scr,
):
    rows = x_ref.shape[1]
    gain = gain_ref[...]

    def lowered(x):
        x = x.astype(F32)
        scale = lax.rsqrt(jnp.mean(x * x, axis=1, keepdims=True) + EPSILON)
        return (x * scale * gain).astype(LOW)

    low_scr[:HALO] = lowered(halo_ref[0])
    low_scr[HALO:] = lowered(x_ref[0])
    low_ref[0] = low_scr[HALO:]
    gate_ref[0] = mm(low_scr[HALO:], main_w[:, :width])
    main_in = mm(low_scr[...], main_w[:, width:]).astype(LOW)
    side_in = mm(low_scr[...], side_w[...])
    mix_scr[:, :width] = main_in.astype(F32)
    mix_scr[:, width:] = side_in[:, : 2 * state].astype(LOW).astype(F32)
    mixed_ref[0] = mix_scr[HALO:].astype(LOW)
    edge_ref[0] = mix_scr[:HALO].astype(LOW)
    conv = taps_ref[CONV : CONV + 1]
    for k in range(CONV):
        at = HALO - (CONV - 1) + k
        conv = conv + taps_ref[k : k + 1] * mix_scr[at : at + rows]
    pre_ref[0] = conv
    active = conv * sigmoid(conv)
    step_arg = side_in[HALO:, 2 * state :] + terms_ref[0:1]
    step = jnp.maximum(step_arg, 0.0) + jnp.log1p(jnp.exp(-jnp.abs(step_arg)))
    step = first_lanes(step, heads)
    slope = first_lanes(sigmoid(step_arg), heads)
    decay2 = step * (terms_ref[1:2] * LOG2E)
    hot = hot_ref[...]
    triangle = lower(block).astype(F32).astype(LOW)
    sub = block // 2
    tri_sub = lower(sub)
    k_scr[:, :sub, sub:block] = jnp.zeros((2, sub, sub), LOW)
    k_scr[:, :sub, block + sub :] = jnp.zeros((2, sub, sub), LOW)
    held = None
    for b in range(rows // block):
        span = slice(b * block, (b + 1) * block)
        run = running_sum(decay2[span], triangle, heads)
        heads_ref[0, span] = step[span] + pltpu.roll(run, SEG, 1) + pltpu.roll(slope[span], 2 * SEG, 1)
        last = run[block - 1 : block]
        toward = jnp.exp2(last - run)
        values = active[span, :width]
        stepped = spread_heads(step[span], hot) * values
        step_low = stepped.astype(LOW)
        step_ref[0, span] = step_low
        inject_h, inject_l = halves(active[span, width : width + state])
        readout_h, readout_l = halves(active[span, width + state :])
        meet = mm_nt(readout_h, inject_h) + mm_nt(readout_l, inject_h) + mm_nt(readout_h, inject_l)
        meet_tiles = {
            (0, 0): jnp.where(tri_sub, meet[:sub, :sub], 0.0),
            (1, 0): meet[sub:, :sub],
            (1, 1): jnp.where(tri_sub, meet[sub:, sub:], 0.0),
        }
        run_t = jnp.transpose(run)
        for pair in range(heads // 2):
            slot = pair % 2
            for j in range(2):
                h = 2 * pair + j
                for (r, c), tile in meet_tiles.items():
                    gap = run[r * sub : (r + 1) * sub, h : h + 1] - run_t[h : h + 1, c * sub : (c + 1) * sub]
                    at = j * block + c * sub
                    k_scr[slot, r * sub : (r + 1) * sub, at : at + sub] = (
                        tile * jnp.exp2(jnp.minimum(gap, 0.0))
                    ).astype(LOW)
            lanes = slice(pair * LANES, (pair + 1) * LANES)
            one, two = pair_split(step_low[:, lanes])
            y_ref[0, span, lanes] = mm(k_scr[slot], jnp.concatenate([one, two], axis=0))
        weighed = (spread_heads(first_lanes(toward, heads), hot) * stepped).astype(LOW)
        gained = mm_tn(inject_h, weighed)
        through = spread_heads(first_lanes(jnp.broadcast_to(jnp.exp2(last), (8, LANES)), heads), hot)
        if held is not None:
            gained = gained + held * through[0:1]
            total_through = total_through * through
        else:
            total_through = through
        held = gained
        state_ref[0, b] = held
    end_ref[0] = held
    through_ref[0] = total_through


def gate_kernel(
    heads, width, state, block,
    y_in, pre_ref, gate_ref, heads_ref, state_ref, back_ref, gain_ref, skip_ref, hot_ref, *refs,
):
    y_ref, enter_ref, stats_ref = refs[-3:]
    rows = y_in.shape[1]
    hot = hot_ref[...]
    enter = decayed = sum(ref[0] for ref in refs[:-3])
    enter_ref[0] = enter
    gain = gain_ref[...]
    skip = skip_ref[...]
    for b in range(rows // block):
        span = slice(b * block, (b + 1) * block)
        run = first_lanes(pltpu.roll(heads_ref[0, span], LANES - SEG, 1), heads)
        grown = spread_heads(first_lanes(jnp.exp2(run), heads), hot)
        pre = pre_ref[0, span]
        active = pre * sigmoid(pre)
        readout_h, readout_l = halves(active[:, width + state :])
        enter_h, enter_l = halves(enter)
        carried = mm(readout_h, enter_h) + mm(readout_l, enter_h) + mm(readout_h, enter_l)
        y = y_in[0, span] + grown * carried
        y_ref[0, span] = y
        decayed = decayed * grown[block - 1 : block]
        enter = state_ref[0, b] + decayed
        scanned = y + skip * active[:, :width]
        gate = gate_ref[0, span]
        gated = scanned * (gate * sigmoid(gate))
        squares = jnp.sum(gated * gated, axis=1, keepdims=True)
        inner = jnp.sum(gated * (back_ref[0, span] * gain), axis=1, keepdims=True)
        lane = lane_of((block, LANES))
        stats = jnp.where(lane == 0, squares, jnp.where(lane == 1, inner, 0.0))
        stats_ref[0, :, span] = jnp.transpose(stats)[:8]


def out_kernel(
    heads, width, state, block, inner_total, rank_ref,
    y_ref, pre_ref, gate_ref, heads_ref, back_ref, stats_ref, gain_ref, skip_ref, hot_ref,
    normed_ref, grad_y_ref, grad_gate_ref, adjoint_ref, sums_ref, *out_refs,
):
    rows = y_ref.shape[1]

    @pl.when(pl.program_id(0) == 0)
    def _():
        sums_ref[...] = jnp.zeros_like(sums_ref)

    hot = hot_ref[...]
    gain = gain_ref[...]
    skip = skip_ref[...]
    held = None
    for b in reversed(range(rows // block)):
        span = slice(b * block, (b + 1) * block)
        total = jnp.sum(stats_ref[:, 0, :, span], axis=0)
        total = jnp.transpose(jnp.concatenate([total, jnp.zeros((LANES - 8, block), F32)], axis=0))
        scale = lax.rsqrt(total[:, 0:1] / inner_total + EPSILON)
        bend = scale * scale * scale * (total[:, 1:2] / inner_total)
        pre = pre_ref[0, span]
        active = pre * sigmoid(pre)
        values = active[:, :width]
        scanned = y_ref[0, span] + skip * values
        gate = gate_ref[0, span]
        sig = sigmoid(gate)
        gate_act = gate * sig
        gated = scanned * gate_act
        normed = (gated * scale * gain).astype(LOW)
        normed_ref[0, span] = normed
        back = back_ref[0, span]
        grad_gated = scale * (back * gain) - gated * bend
        grad_y = grad_gated * gate_act
        grad_y_ref[0, span] = grad_y
        grad_gate_ref[0, span] = (grad_gated * scanned * (sig * (1.0 + gate * (1.0 - sig)))).astype(LOW)
        sums_ref[:8] += row_sums(back * gated * scale)
        sums_ref[8:] += row_sums(grad_y * values)
        run = first_lanes(pltpu.roll(heads_ref[0, span], LANES - SEG, 1), heads)
        grown = spread_heads(first_lanes(jnp.exp2(run), heads), hot)
        gained = mm_tn(active[:, width + state :].astype(LOW), (grown * grad_y).astype(LOW))
        if held is not None:
            gained = gained + held * grown[block - 1 : block]
        held = gained
        adjoint_ref[0, b] = held
    by_rank(normed_ref[0], rank_ref[0], out_refs)


def back_kernel(
    heads, width, state, block,
    y_ref, pre_ref, mixed_ref, edge_ref, heads_ref, step_ref, grad_y_ref, enter_ref, state_ref, adjoint_ref,
    taps_ref, terms_ref, skip_ref, hot_ref, hot_t_ref, *refs,
):
    leave_refs, refs = refs[:-10], refs[-10:]
    (
    grad_mixed_ref, grad_step_ref, head_ref, tail_ref, filter_ref, terms_out_ref,
    k_scr, u_scr, cross_scr, conv_scr,
    ) = refs
    rows = y_ref.shape[1]
    blocks = rows // block

    @pl.when(pl.program_id(0) == 0)
    def _():
        filter_ref[...] = jnp.zeros_like(filter_ref)
        terms_out_ref[...] = jnp.zeros_like(terms_out_ref)

    hot = hot_ref[...]
    hot_t = hot_t_ref[...]
    skip = skip_ref[...]
    sub = block // 2
    tri = lower(block)
    upper_sub = jnp.logical_not(lower(sub)) | (
        lax.broadcasted_iota(jnp.int32, (sub, sub), 0) == lane_of((sub, sub))
    )
    upper = jnp.logical_not(tri) | (
        lax.broadcasted_iota(jnp.int32, (block, block), 0) == lane_of((block, block))
    )
    suffix = upper.astype(F32).astype(LOW)
    rate = terms_ref[1:2]
    k_scr[:, sub:, :sub] = jnp.zeros((2, sub, sub), LOW)
    k_scr[:, sub:, block : block + sub] = jnp.zeros((2, sub, sub), LOW)
    conv_scr[:HALO] = jnp.zeros((HALO, conv_scr.shape[1]), F32)
    conv_scr[HALO + rows :] = jnp.zeros((HALO, conv_scr.shape[1]), F32)
    leave = sum(ref[0].astype(F32) for ref in leave_refs)
    runs = [first_lanes(pltpu.roll(heads_ref[0, b * block : (b + 1) * block], LANES - SEG, 1), heads) for b in range(blocks)]
    enters = [enter_ref[0]]
    decayed = enter_ref[0]
    for b in range(blocks):
        last = jnp.broadcast_to(jnp.exp2(runs[b][block - 1 : block]), (8, LANES))
        decayed = decayed * spread_heads(first_lanes(last, heads), hot)[0:1]
        enters.append(state_ref[0, b] + decayed)
    for b in reversed(range(blocks)):
        span = slice(b * block, (b + 1) * block)
        packed = heads_ref[0, span]
        step = first_lanes(packed, heads)
        slope_step = first_lanes(pltpu.roll(packed, LANES - 2 * SEG, 1), heads)
        run = runs[b]
        last = run[block - 1 : block]
        pre = pre_ref[0, span]
        sig = sigmoid(pre)
        active = pre * sig
        slope = sig * (1.0 + pre * (1.0 - sig))
        values = active[:, :width]
        inject_h, inject_l = halves(active[:, width : width + state])
        readout_h, readout_l = halves(active[:, width + state :])
        step_low = step_ref[0, span]
        grad_y = grad_y_ref[0, span]
        grad_low = grad_y.astype(LOW)
        leave_low = leave.astype(LOW)
        toward = spread_heads(first_lanes(jnp.exp2(last - run), heads), hot)
        grown = spread_heads(first_lanes(jnp.exp2(run), heads), hot)
        grown_h, grown_l = halves(grown * grad_y)
        u_scr[...] = toward * mm(inject_h, leave_low)
        meet = mm_nt(inject_h, readout_h) + mm_nt(inject_h, readout_l) + mm_nt(inject_l, readout_h)
        meet_tiles = {
            (0, 0): jnp.where(upper_sub, meet[:sub, :sub], 0.0),
            (0, 1): meet[:sub, sub:],
            (1, 1): jnp.where(upper_sub, meet[sub:, sub:], 0.0),
        }
        run_t = jnp.transpose(run)
        cross_scr[...] = jnp.zeros_like(cross_scr)
        for pair in range(heads // 2):
            slot = pair % 2
            lanes = slice(pair * LANES, (pair + 1) * LANES)
            tile_low = step_low[:, lanes]
            split = pair_split(grad_low[:, lanes])
            for j in range(2):
                h = 2 * pair + j
                products = {}
                top = mm_nt(tile_low[:sub], split[j])
                products[(0, 0)] = top[:, :sub]
                products[(0, 1)] = top[:, sub:]
                products[(1, 1)] = mm_nt(tile_low[sub:], split[j][sub:])
                for (r, c), tile in meet_tiles.items():
                    gap = run_t[h : h + 1, c * sub : (c + 1) * sub] - run[r * sub : (r + 1) * sub, h : h + 1]
                    fall = jnp.exp2(jnp.minimum(gap, 0.0))
                    at = j * block + c * sub
                    k_scr[slot, r * sub : (r + 1) * sub, at : at + sub] = (tile * fall).astype(LOW)
                    cross_scr[r * sub : (r + 1) * sub, c * sub : (c + 1) * sub] += fall * products[(r, c)]
            u_scr[:, lanes] += mm(k_scr[slot], jnp.concatenate(split, axis=0))
        cross = jnp.where(upper, cross_scr[...], 0.0).astype(LOW)
        enter_h, enter_l = halves(enters[b])
        grad_readout = (
            mm_tn(cross, inject_h) + mm_nt(grown_h, enter_h) + mm_nt(grown_l, enter_h) + mm_nt(grown_h, enter_l)
        )
        weighed = (toward * step_low.astype(F32)).astype(LOW)
        grad_inject = mm(cross, readout_h) + mm_nt(weighed, leave_low)
        u = u_scr[...]
        grad_step = sum_heads(values * u, hot_t)
        taken = step_low.astype(F32) * u
        given = grad_low.astype(F32) * y_ref[0, span]
        flow = running_sum(sum_heads(given - taken, hot_t), suffix, heads)
        ends = jnp.sum(leave * enters[b + 1], axis=0, keepdims=True)
        flow = flow + first_lanes(sum_heads(jnp.broadcast_to(ends, (8, width)), hot_t)[0:1], heads)
        grad_arg = (grad_step + rate * flow) * slope_step
        grad_step_ref[0, span] = grad_arg.astype(LOW)
        terms_out_ref[:8] += row_sums(grad_arg)
        terms_out_ref[8:] += row_sums(flow * step * rate)
        grad_values = spread_heads(step, hot) * u + skip * grad_y
        conv_scr[HALO + b * block : HALO + (b + 1) * block, :width] = grad_values * slope[:, :width]
        conv_scr[HALO + b * block : HALO + (b + 1) * block, width : width + state] = (
            grad_inject * slope[:, width : width + state]
        )
        conv_scr[HALO + b * block : HALO + (b + 1) * block, width + state :] = (
            grad_readout * slope[:, width + state :]
        )
        if b:
            leave = adjoint_ref[0, b] + grown[block - 1 : block] * leave
    head_ref[0] = conv_scr[HALO : HALO + 8]
    mixed = mixed_ref[0].astype(F32)
    edge = edge_ref[0].astype(F32)
    total = None
    for k in range(CONV):
        ahead = CONV - 1 - k
        moved = conv_scr[HALO + ahead : HALO + ahead + rows]
        term = taps_ref[k : k + 1] * moved
        total = term if total is None else total + term
        filter_ref[8 * k : 8 * k + 8] += row_sums(mixed * moved) + row_sums(edge * conv_scr[ahead : ahead + HALO])
    filter_ref[8 * CONV :] += row_sums(conv_scr[HALO : HALO + rows])
    high, least = halves(total)
    grad_mixed_ref[0, :, : width + 2 * state] = high
    grad_mixed_ref[0, :, width + 2 * state :] = least[:, width:]
    tail_ref[0] = total[rows - HALO :]


def top_kernel(rows, first, length_ref, place_ref, cot_ref, out_w, top_ref, back_ref):
    valid = length_ref[first + pl.program_id(0)] - place_ref[0]
    cot = cot_ref[0]
    row = lax.broadcasted_iota(jnp.int32, cot.shape, 0)
    top = jnp.where(row < valid, cot.astype(F32), 0.0).astype(LOW)
    top_ref[0] = top
    back_ref[0] = mm_nt(top, out_w[...])


def by_rank(rows, rank, out_refs):
    share = out_refs[0].shape[0]
    count = rows.shape[0] // share
    for k in range(count):
        place = (pl.program_id(0) * count + k) ^ rank
        for d in range(len(out_refs)):

            @pl.when(place == d)
            def _(k=k, d=d):
                out_refs[d][...] = rows[k * share : (k + 1) * share]


def lowered_kernel(width, state, gate_ref, mixed_ref, step_ref, main_w, side_w, out_ref):
    main = jnp.concatenate([gate_ref[0], mixed_ref[0, :, :width]], axis=1)
    side = jnp.concatenate([mixed_ref[0, :, width : width + 2 * state], step_ref[0]], axis=1)
    out_ref[0] = (mm_nt(main, main_w[...]) + mm_nt(side, side_w[...])).astype(LOW)


def product_kernel(ranks, rank_ref, *refs):
    x_refs, weight_ref = refs[:STREAMS], refs[STREAMS]
    parts = refs[STREAMS + 1 : -2]
    out_ref, acc_ref = refs[-2:]
    share = parts[0].shape[0]
    at = pl.program_id(0)
    for d in range(ranks):

        @pl.when(at == d)
        def _(d=d):
            rows = jnp.concatenate([parts[s * ranks + d][...] for s in range(STREAMS)], axis=0)
            part = mm(rows, weight_ref[0])
            if d == 0:
                part = part + jnp.concatenate([x[0].astype(F32) for x in x_refs], axis=0)
            else:
                part = part + acc_ref[...]
            acc_ref[...] = part

    @pl.when(at == ranks - 1)
    def _():
        for s in range(STREAMS):
            out_ref[s] = acc_ref[s * share : (s + 1) * share].astype(LOW)


def hand_kernel(local_ref, through_ref, arrived_ref, out_ref):
    out_ref[0] = local_ref[0] + through_ref[0, :1] * arrived_ref[0]


def place_kernel(block_ref, out_ref):
    out_ref[...] = block_ref[...]


def merged(ref):
    return ref[...].reshape(ref.shape[0] * ref.shape[1], ref.shape[2])


def lane_sums(a):
    return sum(a[:, k : k + LANES] for k in range(0, a.shape[1], LANES))


def gate_grad_kernel(*refs):
    low, grads = refs[:STREAMS], refs[STREAMS : 2 * STREAMS]
    main_w, out_ref, gain_ref = refs[2 * STREAMS :]
    gate = sum(mm_tn(merged(a), merged(b)) for a, b in zip(low, grads))
    out_ref[...] = gate.astype(LOW)
    gain_ref[...] = lane_sums(main_w[...].astype(F32) * gate)


def out_grad_kernel(*refs):
    normed, top, out_ref = refs[:STREAMS], refs[STREAMS : 2 * STREAMS], refs[-1]
    out_ref[...] = sum(mm_tn(merged(a), merged(b)) for a, b in zip(normed, top)).astype(LOW)


def late_kernel(width, state, *refs):
    low, mixed, step = (refs[k * STREAMS : (k + 1) * STREAMS] for k in range(3))
    main_w, side_w, gain_in, own_ref, shared_ref, gain_ref = refs[3 * STREAMS :]
    total = sum(mm_tn(merged(a), merged(b)) for a, b in zip(low, mixed))
    steps = sum(mm_tn(merged(a), merged(b)) for a, b in zip(low, step))
    main = total[:, :width]
    shared = total[:, width : width + 2 * state] + total[:, width + 2 * state :]
    own_ref[:, :width] = main.astype(LOW)
    own_ref[:, width:] = steps.astype(LOW)
    shared_ref[...] = shared
    side = side_w[...].astype(F32)
    gain_ref[...] = (
        gain_in[...]
        + lane_sums(main_w[...].astype(F32) * main)
        + lane_sums(side[:, : 2 * state] * shared)
        + side[:, 2 * state :] * steps
    )


def by_rank(rows, rank, out_refs):
    share = out_refs[0].shape[0]
    count = rows.shape[0] // share
    for k in range(count):
        place = (pl.program_id(0) * count + k) ^ rank
        for d in range(len(out_refs)):

            @pl.when(place == d)
            def _(k=k, d=d):
                out_refs[d][...] = rows[k * share : (k + 1) * share]


def lowered_kernel(width, state, rank_ref, gate_ref, mixed_ref, step_ref, main_w, side_w, *out_refs):
    main = jnp.concatenate([gate_ref[0], mixed_ref[0, :, :width]], axis=1)
    side = jnp.concatenate([mixed_ref[0, :, width : width + 2 * state], step_ref[0]], axis=1)
    total = (mm_nt(main, main_w[...]) + mm_nt(side, side_w[...])).astype(LOW)
    by_rank(total, rank_ref[0], out_refs)


def norm_kernel(ranks, rank_ref, x_ref, top_ref, gain_ref, *refs):
    out_ref = refs[ranks]
    x = x_ref[0].astype(F32)
    scale = lax.rsqrt(jnp.mean(x * x, axis=1, keepdims=True) + EPSILON)
    normed = x * scale
    grad = sum(ref[...].astype(F32) for ref in refs[:ranks])
    scaled = grad * gain_ref[...]
    out = top_ref[0].astype(F32) + scale * (scaled - normed * jnp.mean(scaled * normed, axis=1, keepdims=True))
    out_ref[...] = out.astype(LOW)


def ignoring(kernel, first, count):
    def body(*refs):
        kernel(*refs[:first], *refs[first + count :])

    return body


def per_device(
    residual_in,
    lengths,
    input_gain,
    main_in_weight,
    weight_shared,
    step_in_weight,
    filter_main,
    filter_shared,
    head_terms,
    output_gain,
    out_projection_weight,
    cotangent,
):
    all_seqs, rows, model = residual_in.shape
    seqs = all_seqs // STREAMS
    heads = step_in_weight.shape[1]
    width = main_in_weight.shape[2]
    state = weight_shared.shape[1] // 2
    mixed_width = width + 2 * state
    kept_width = mixed_width + 2 * state
    ranks = lax.axis_size("tensor")
    spans = lax.axis_size("seq")
    inner_total = width * ranks
    reach = CONV - 1
    block = min(BLOCK_LEN, rows)
    blocks = rows // block
    share = seqs * rows // ranks
    sds = jax.ShapeDtypeStruct

    main_w = main_in_weight.reshape(model, 2 * width)
    side_w = jnp.concatenate(
        [weight_shared, jnp.pad(step_in_weight, ((0, 0), (0, LANES - heads)))], axis=1
    )
    side_width = side_w.shape[1]
    taps = jnp.pad(jnp.concatenate([filter_main, filter_shared], axis=1), ((0, 8 - CONV - 1), (0, 0)))
    rate = -jnp.exp(head_terms[1])
    terms = jnp.pad(jnp.stack([head_terms[0], rate]), ((0, 6), (0, LANES - heads)))
    skip = jnp.repeat(head_terms[2], HEADDIM)[None]
    channel_head = jnp.arange(width, dtype=jnp.int32)[None, :] // HEADDIM
    lane = jnp.arange(LANES, dtype=jnp.int32)[:, None]
    hot = ((lane % SEG == channel_head) & (lane < 3 * SEG)).astype(LOW)
    hot_t = (lane == channel_head).astype(LOW).T
    in_gain = input_gain[None]
    out_gain = output_gain[None]
    dims = (heads, width, state, block)
    place = (lax.axis_index("seq") * rows).astype(jnp.int32)[None]
    rank = lax.axis_index("tensor").astype(jnp.int32)[None]
    halo = shifted(residual_in[:, rows - HALO :, :], "seq", 1)
    full_w = lax.all_gather(out_projection_weight, "tensor", axis=0)
    smem = pl.BlockSpec(memory_space=pltpu.SMEM)
    anywhere = pl.BlockSpec(memory_space=pl.ANY)

    def cost(flops):
        return pl.CostEstimate(flops=int(flops), bytes_accessed=30 << 20, transcendentals=0)

    def project(s, halo, marks=()):
        return pl.pallas_call(
            ignoring(functools.partial(project_kernel, *dims), 8, len(marks)),
            grid=(seqs,),
            in_specs=[
                per_seq(rows, model, offset=s * seqs), per_seq(HALO, model, offset=s * seqs), whole((1, model)),
                whole((model, 2 * width)), whole((model, side_width)), whole((8, mixed_width)), whole((8, LANES)),
                whole((LANES, width)),
            ]
            + [anywhere] * len(marks),
            out_specs=[
                per_seq(rows, model), per_seq(rows, mixed_width), per_seq(HALO, mixed_width),
                per_seq(rows, mixed_width), per_seq(rows, width), per_seq(rows, LANES), per_seq(rows, width),
                per_seq(rows, width), per_seq(blocks, state, width), per_seq(state, width), per_seq(8, width),
            ],
            out_shape=[
                sds((seqs, rows, model), LOW), sds((seqs, rows, mixed_width), LOW),
                sds((seqs, HALO, mixed_width), LOW), sds((seqs, rows, mixed_width), F32),
                sds((seqs, rows, width), F32), sds((seqs, rows, LANES), F32), sds((seqs, rows, width), LOW),
                sds((seqs, rows, width), F32), sds((seqs, blocks, state, width), F32),
                sds((seqs, state, width), F32), sds((seqs, 8, width), F32),
            ],
            scratch_shapes=[
                pltpu.VMEM((HALO + rows, model), LOW), pltpu.VMEM((HALO + rows, mixed_width), F32),
                pltpu.VMEM((2, block, 2 * block), LOW),
            ],
            compiler_params=params(),
            cost_estimate=cost(8e9 * seqs),
            name="project",
        )(residual_in, halo, in_gain, main_w, side_w, taps, terms, hot, *marks)

    def handed(local, through, arrived, marks):
        return pl.pallas_call(
            ignoring(hand_kernel, 3, len(marks)),
            grid=(seqs,),
            in_specs=[per_seq(state, width), per_seq(8, width), per_seq(state, width)] + [anywhere] * len(marks),
            out_specs=per_seq(state, width),
            out_shape=sds((seqs, state, width), F32),
            compiler_params=params(),
            name="handed",
        )(local, through, arrived, *marks)

    def chained(local, through, direction, kind, marks=None):
        arrivals = []
        for hop in range(spans - 1):
            sender = hop if direction > 0 else spans - 1 - hop
            if hop == 0:
                sent = local
            elif marks:
                sent = handed(local, through, arrivals[-1], marks[min(hop, len(marks)) - 1])
            else:
                sent = local + through[:, :1] * arrivals[-1].astype(F32)
            arrivals.append(lax.ppermute(sent.astype(kind), "seq", [(sender, sender + direction)]))
        return arrivals

    def top_of(s, place, marks=()):
        return pl.pallas_call(
            ignoring(functools.partial(top_kernel, rows, s * seqs), 4, len(marks)),
            grid=(seqs,),
            in_specs=[smem, smem, per_seq(rows, model, offset=s * seqs), whole((width, model))]
            + [anywhere] * len(marks),
            out_specs=[per_seq(rows, model), per_seq(rows, width)],
            out_shape=[sds((seqs, rows, model), LOW), sds((seqs, rows, width), F32)],
            compiler_params=params(),
            cost_estimate=cost(2.5e9 * seqs),
            name="top",
        )(lengths, place, cotangent, out_projection_weight, *marks)

    def gated_of(y_local, pre, gate, packed, arrivals, states, back, marks=()):
        return pl.pallas_call(
            ignoring(functools.partial(gate_kernel, *dims), 9 + len(arrivals), len(marks)),
            grid=(seqs,),
            in_specs=[
                per_seq(rows, width), per_seq(rows, mixed_width), per_seq(rows, width), per_seq(rows, LANES),
                per_seq(blocks, state, width), per_seq(rows, width), whole((1, width)),
                whole((1, width)), whole((LANES, width)),
            ]
            + [per_seq(state, width)] * len(arrivals)
            + [anywhere] * len(marks),
            out_specs=[per_seq(rows, width), per_seq(state, width), per_seq(8, rows)],
            out_shape=[sds((seqs, rows, width), F32), sds((seqs, state, width), F32), sds((seqs, 8, rows), F32)],
            compiler_params=params(),
            cost_estimate=cost(4e9 * seqs),
            name="gated",
        )(y_local, pre, gate, packed, states, back, out_gain, skip, hot, *arrivals, *marks)

    def outward(y, pre, gate, packed, back, all_stats, marks=()):
        seq = lambda *shape: pl.BlockSpec((1,) + shape, lambda i, r: (i,) + (0,) * len(shape))
        fixed = lambda *shape: pl.BlockSpec(shape, lambda i, r: (0,) * len(shape))
        return pl.pallas_call(
            ignoring(functools.partial(out_kernel, *dims, inner_total), 10, len(marks)),
            grid_spec=pltpu.PrefetchScalarGridSpec(
                num_scalar_prefetch=1,
                grid=(seqs,),
                in_specs=[
                    seq(rows, width), seq(rows, mixed_width), seq(rows, width), seq(rows, LANES), seq(rows, width),
                    pl.BlockSpec((ranks, 1, 8, rows), lambda i, r: (0, i, 0, 0)), fixed(1, width), fixed(1, width),
                    fixed(LANES, width),
                ]
                + [anywhere] * len(marks),
                out_specs=[
                    seq(rows, width), seq(rows, width), seq(rows, width), seq(blocks, state, width), fixed(16, width),
                ]
                + [fixed(share, width)] * ranks,
            ),
            out_shape=[
                sds((seqs, rows, width), LOW), sds((seqs, rows, width), F32), sds((seqs, rows, width), LOW),
                sds((seqs, blocks, state, width), F32), sds((16, width), F32),
            ]
            + [sds((share, width), LOW)] * ranks,
            compiler_params=params(),
            cost_estimate=cost(5e9 * seqs),
            name="outward",
        )(rank, y, pre, gate, packed, back, all_stats, out_gain, skip, hot, *marks)

    def backward(marks, y, pre, mixed, edge, packed, stepped, grad_y, entering, states, leaving, adjoint):
        return pl.pallas_call(
            ignoring(functools.partial(back_kernel, *dims), 15 + len(leaving), len(marks)),
            grid=(seqs,),
            in_specs=[
                per_seq(rows, width), per_seq(rows, mixed_width), per_seq(rows, mixed_width),
                per_seq(HALO, mixed_width), per_seq(rows, LANES), per_seq(rows, width), per_seq(rows, width),
                per_seq(state, width), per_seq(blocks, state, width),
                per_seq(blocks, state, width), whole((8, mixed_width)), whole((8, LANES)), whole((1, width)),
                whole((LANES, width)), whole((width, LANES)),
            ]
            + [per_seq(state, width)] * len(leaving)
            + [anywhere] * len(marks),
            out_specs=[
                per_seq(rows, kept_width), per_seq(rows, LANES), per_seq(8, mixed_width), per_seq(HALO, mixed_width),
                pl.BlockSpec((8 * (CONV + 1), mixed_width), lambda i: (0, 0)),
                pl.BlockSpec((16, LANES), lambda i: (0, 0)),
            ],
            out_shape=[
                sds((seqs, rows, kept_width), LOW), sds((seqs, rows, LANES), LOW), sds((seqs, 8, mixed_width), F32),
                sds((seqs, HALO, mixed_width), F32), sds((8 * (CONV + 1), mixed_width), F32), sds((16, LANES), F32),
            ],
            scratch_shapes=[
                pltpu.VMEM((2, block, 2 * block), LOW), pltpu.VMEM((block, width), F32),
                pltpu.VMEM((block, block), F32), pltpu.VMEM((2 * HALO + rows, mixed_width), F32),
            ],
            compiler_params=params(),
            cost_estimate=cost(11e9 * seqs),
            name="backward",
        )(
            y, pre, mixed, edge, packed, stepped, grad_y, entering, states, adjoint,
            taps, terms, skip, hot, hot_t, *leaving, *marks,
        )

    def lowered_of(grad_gate, grad_mixed, grad_step, marks=()):
        seq = lambda *shape: pl.BlockSpec((1,) + shape, lambda i, r: (i,) + (0,) * len(shape))
        fixed = lambda *shape: pl.BlockSpec(shape, lambda i, r: (0,) * len(shape), pipeline_mode=pl.Buffered(1))
        return pl.pallas_call(
            ignoring(functools.partial(lowered_kernel, width, state), 6, len(marks)),
            grid_spec=pltpu.PrefetchScalarGridSpec(
                num_scalar_prefetch=1,
                grid=(seqs,),
                in_specs=[
                    seq(rows, width), seq(rows, kept_width), seq(rows, LANES), fixed(model, 2 * width),
                    fixed(model, side_width),
                ]
                + [anywhere] * len(marks),
                out_specs=[pl.BlockSpec((share, model), lambda i, r: (0, 0))] * ranks,
            ),
            out_shape=[sds((share, model), LOW)] * ranks,
            compiler_params=params(),
            cost_estimate=cost(4.5e9 * seqs),
            name="lowered",
        )(rank, grad_gate, grad_mixed, grad_step, main_w, side_w, *marks)

    def input_norm(s, parts, top, marks=()):
        return pl.pallas_call(
            ignoring(functools.partial(norm_kernel, ranks), 4 + len(parts), len(marks)),
            grid_spec=pltpu.PrefetchScalarGridSpec(
                num_scalar_prefetch=1,
                grid=(1,),
                in_specs=[
                    pl.BlockSpec((1, share, model), lambda i, r: (s * ranks + r[0], 0, 0)),
                    pl.BlockSpec((1, share, model), lambda i, r: (r[0], 0, 0)),
                    pl.BlockSpec((1, model), lambda i, r: (0, 0)),
                ]
                + [pl.BlockSpec((share, model), lambda i, r: (0, 0))] * ranks
                + [anywhere] * len(marks),
                out_specs=pl.BlockSpec((share, model), lambda i, r: (0, 0)),
            ),
            out_shape=sds((share, model), LOW),
            compiler_params=params(),
            name="input_norm",
        )(rank, residual_in.reshape(-1, share, model), top.reshape(-1, share, model), in_gain, *parts, *marks)

    def product(parts, marks=()):
        row_of = lambda s: pl.BlockSpec((1, share, model), lambda i, r: (s * ranks + r[0], 0, 0))
        x = residual_in.reshape(-1, share, model)
        return pl.pallas_call(
            ignoring(functools.partial(product_kernel, ranks), 2 + STREAMS + len(parts), len(marks)),
            grid_spec=pltpu.PrefetchScalarGridSpec(
                num_scalar_prefetch=1,
                grid=(ranks,),
                in_specs=[row_of(s) for s in range(STREAMS)]
                + [pl.BlockSpec((1, width, model), lambda i, r: (r[0] ^ i, 0, 0))]
                + [pl.BlockSpec((share, width), lambda i, r: (0, 0))] * (STREAMS * ranks)
                + [anywhere] * len(marks),
                out_specs=pl.BlockSpec((STREAMS, share, model), lambda i, r: (0, 0, 0)),
                scratch_shapes=[pltpu.VMEM((STREAMS * share, model), F32)],
            ),
            out_shape=sds((STREAMS, share, model), LOW),
            compiler_params=params(),
            cost_estimate=cost(2.4e9 * all_seqs),
            name="product",
        )(rank, *[x] * STREAMS, full_w, *parts, *marks)

    tile = 256
    tiles = model // tile
    column = pl.BlockSpec((seqs, rows, tile), lambda i: (0, 0, i))
    row = lambda n: pl.BlockSpec((tile, n), lambda i: (i, 0))

    def gate_grad(low, grads, marks=()):
        return pl.pallas_call(
            ignoring(gate_grad_kernel, 2 * STREAMS + 1, len(marks)),
            grid=(tiles,),
            in_specs=[column] * STREAMS + [whole((seqs, rows, width))] * STREAMS + [row(width)]
            + [anywhere] * len(marks),
            out_specs=[row(width), row(LANES)],
            out_shape=[sds((model, width), LOW), sds((model, LANES), F32)],
            compiler_params=params(),
            cost_estimate=cost(2.5e9 * all_seqs),
            name="gate_grad",
        )(*low, *grads, main_w, *marks)

    def out_grad(normed, top, marks=()):
        return pl.pallas_call(
            ignoring(out_grad_kernel, 2 * STREAMS, len(marks)),
            grid=(width // tile,),
            in_specs=[column] * STREAMS + [whole((seqs, rows, model))] * STREAMS + [anywhere] * len(marks),
            out_specs=row(model),
            out_shape=sds((width, model), LOW),
            compiler_params=params(),
            cost_estimate=cost(2.5e9 * all_seqs),
            name="out_grad",
        )(*normed, *top, *marks)

    def late_of(low, mixed, step, gain, marks=()):
        return pl.pallas_call(
            ignoring(functools.partial(late_kernel, width, state), 3 * STREAMS + 3, len(marks)),
            grid=(tiles,),
            in_specs=[column] * STREAMS
            + [whole((seqs, rows, kept_width))] * STREAMS
            + [whole((seqs, rows, LANES))] * STREAMS
            + [pl.BlockSpec((tile, width), lambda i: (i, 1)), row(side_width), row(LANES)]
            + [anywhere] * len(marks),
            out_specs=[row(width + LANES), row(2 * state), row(LANES)],
            out_shape=[sds((model, width + LANES), LOW), sds((model, 2 * state), F32), sds((model, LANES), F32)],
            compiler_params=params(),
            cost_estimate=cost(5e9 * all_seqs),
            name="late",
        )(*low, *mixed, *step, main_w, side_w, gain, *marks)

    def exchanged(own):
        return [own] + [
            lax.ppermute(own, "tensor", [(i, i ^ d) for i in range(ranks)]) for d in range(1, ranks)
        ]

    def swapped(blocks_of):
        return [
            lax.ppermute(b, "tensor", [(i, i ^ d) for i in range(ranks)]) if d else b for d, b in enumerate(blocks_of)
        ]

    def scattered(whole_rows):
        blocks_of = whole_rows.reshape(ranks, share, -1)
        return swapped([lax.dynamic_index_in_dim(blocks_of, rank[0] ^ d, axis=0, keepdims=False) for d in range(ranks)])

    def placed(blocks, total, marks):
        count = blocks.shape[0]
        return pl.pallas_call(
            ignoring(place_kernel, 1, len(marks)),
            grid=(count // 2,),
            in_specs=[pl.BlockSpec((2, share, model), lambda i: (i, 0, 0))] + [anywhere] * len(marks),
            out_specs=pl.BlockSpec((2, share, model), lambda i: (i, 0, 0)),
            out_shape=sds((total, share, model), LOW),
            compiler_params=params(),
            name="placed",
        )(blocks, *marks)

    def assembled(held, pieces, marks):
        total = held.shape[0]

        def kernel(rank_ref, held_ref, *refs):
            out_ref, sems = refs[ranks:]
            copies = [
                pltpu.make_async_copy(refs[d], out_ref.at[total - ranks + (rank_ref[0] ^ d)], sems.at[d])
                for d in range(ranks)
            ]
            for copy in copies:
                copy.start()
            for copy in copies:
                copy.wait()

        return pl.pallas_call(
            ignoring(kernel, 2 + ranks, len(marks)),
            in_specs=[smem, anywhere] + [pl.BlockSpec(memory_space=pltpu.VMEM)] * ranks + [anywhere] * len(marks),
            out_specs=anywhere,
            out_shape=sds((total, share, model), LOW),
            input_output_aliases={1: 0},
            scratch_shapes=[pltpu.SemaphoreType.DMA((ranks,))],
            compiler_params=pltpu.CompilerParams(vmem_limit_bytes=VMEM),
            name="assemble",
        )(rank, held, *pieces, *marks)

    flat = lambda a: a.reshape(seqs * rows, a.shape[-1])
    both = range(STREAMS)

    def backward_of(s, leaving, marks, fill):
        made, step_low, head, tail, filter_sum, term_sum = backward(
            marks, y[s], pre[s], mixed[s], edge[s], packed[s], stepped[s], grad_y[s], entering[s], states[s],
            leaving, adjoint[s],
        )
        following = shifted(head[:, :reach], "seq", -1)
        fill(step_low)
        fix = jnp.zeros((seqs, reach, mixed_width), F32)
        for k in range(reach):
            fix = fix + jnp.pad(taps[k] * following[:, : reach - k], ((0, 0), (k, 0), (0, 0)))
        tail = tail + jnp.pad(fix, ((0, 0), (HALO - reach, 0), (0, 0)))
        tail_high = tail.astype(LOW)
        tail_least = (tail - lax.optimization_barrier(tail_high).astype(F32)).astype(LOW)[:, :, width:]
        made = lax.dynamic_update_slice(
            made, jnp.concatenate([tail_high, tail_least], axis=2), (0, rows - HALO, 0)
        )
        return made, step_low, filter_sum, term_sum

    reduced = lambda a, axis=0: lax.psum_scatter(a, ("seq", "dp"), scatter_dimension=axis, tiled=True)

    first = [project(0, halo)]
    first.append(project(1, halo, [first[0][-1]]))
    low, mixed, edge, pre, gate, packed, stepped, y_local, states, local, through = zip(*first)
    tops = [top_of(0, place, [through[1]])]
    tops.append(top_of(1, place, [tops[0][0]]))
    top, back = zip(*tops)

    def gated_of_stream(s, arrivals, marks):
        y, entering, stats = gated_of(y_local[s], pre[s], gate[s], packed[s], arrivals, states[s], back[s], marks)
        return y, entering, stats, lax.all_gather(stats, "tensor", axis=0)

    y, entering, stats, all_stats = [None] * 2, [None] * 2, [None] * 2, [None] * 2
    second = []
    arrivals = chained(local[0], through[0], 1, F32)
    y[0], entering[0], stats[0], all_stats[0] = gated_of_stream(0, arrivals, [top[1]])
    second.append(outward(y[0], pre[0], gate[0], packed[0], back[0], all_stats[0]))
    arrivals = chained(local[1], through[1], 1, F32)
    y[1], entering[1], stats[1], all_stats[1] = gated_of_stream(1, arrivals, [second[0][0]])
    parts = swapped(second[0][5:])
    leaving = [chained(second[0][3][:, 0], through[0], -1, LOW)]
    second.append(outward(y[1], pre[1], gate[1], packed[1], back[1], all_stats[1], [leaving[0][0]]))
    normed, grad_y, grad_gate, adjoint, out_sums = list(zip(*second))[:5]
    leaving.append(chained(adjoint[1][:, 0], through[1], -1, LOW))
    gate_w, gain_sums = gate_grad(low, grad_gate, [normed[1], leaving[0][1]])
    gate_w_sum = reduced(gate_w)
    made_out = product(parts + swapped(second[1][5:]), [gate_w, leaving[1][0]])
    block_out = lax.all_gather(made_out, "tensor", axis=1, tiled=True)
    out_w = []
    third = [
        backward_of(0, leaving[0], [made_out, leaving[1][1]], lambda raw: out_w.append(out_grad(normed, top, [raw])))
    ]
    out_w_sum = reduced(out_w[0], 1)
    partial = [lowered_of(grad_gate[0], *third[0][:2], [out_w[0]])]
    sums = [swapped(partial[0])]
    own = []
    third.append(
        backward_of(
            1, leaving[1], [partial[0][0], block_out], lambda raw: own.append(input_norm(0, sums[0], top[0], [raw]))
        )
    )
    first_in = lax.all_gather(own[0], "tensor", axis=0, tiled=True)
    grad_mixed, grad_step, filter_sums, term_sums = zip(*third)
    grad_own, grad_side, gain_sums = late_of(low, grad_mixed, grad_step, gain_sums, [own[0]])
    partial.append(lowered_of(grad_gate[1], *third[1][:2], [grad_own, gate_w_sum]))
    sums.append(swapped(partial[1]))
    own_sum = reduced(grad_own)
    grad_own_w = own_sum.astype(F32)
    shared_w = reduced(grad_side)
    grad_gate_w = gate_w_sum.astype(F32)
    grad_out_w = out_w_sum.astype(F32)
    grad_main_w = jnp.stack([grad_gate_w, grad_own_w[:, :width]], axis=1)
    grad_step_w = grad_own_w[:, width : width + heads]
    filters = jnp.sum(sum(filter_sums).reshape(CONV + 1, 8, mixed_width), axis=1)
    term_rows = jnp.sum(sum(term_sums).reshape(2, 8, LANES), axis=1)
    out_rows = jnp.sum(sum(out_sums).reshape(2, 8, width), axis=1)
    grad_skip = jnp.pad(jnp.sum(out_rows[1].reshape(heads, HEADDIM), axis=1), (0, LANES - heads))
    everywhere = (jnp.sum(gain_sums, axis=1) / input_gain, filters[:, width:])
    per_rank = (filters[:, :width], jnp.concatenate([term_rows, grad_skip[None]], axis=0), out_rows[0])
    packed_sums = jnp.concatenate([a.reshape(-1) for a in everywhere + per_rank])
    packed_sums = jnp.sum(lax.all_gather(packed_sums.reshape(-1, LANES), ("seq", "dp"), axis=0), axis=0)
    split = (everywhere[0].size + everywhere[1].size) // LANES
    shared_sums = jnp.sum(lax.all_gather(packed_sums[:split], "tensor", axis=0), axis=0).reshape(-1)
    rank_sums = packed_sums[split:].reshape(-1)
    small_in = shared_sums[:model]
    small_shared = shared_sums[model:].reshape(CONV + 1, 2 * state)
    small_main = rank_sums[: (CONV + 1) * width].reshape(CONV + 1, width)
    small_terms = rank_sums[(CONV + 1) * width : -width].reshape(3, LANES)[:, :heads]
    small_out = rank_sums[-width:]
    last_own = input_norm(1, sums[1], top[1], [shared_sums, first_in])
    pieces = exchanged(last_own)
    stacked = STREAMS * ranks
    block_out = placed(block_out.reshape(stacked, share, model), stacked, [last_own])
    input_grad = placed(first_in.reshape(-1, share, model), stacked, [last_own, block_out])
    shared_w = pl.pallas_call(
        ignoring(place_kernel, 1, 2),
        in_specs=[pl.BlockSpec(memory_space=pltpu.VMEM), anywhere, anywhere],
        out_specs=pl.BlockSpec(memory_space=pltpu.VMEM),
        out_shape=sds(shared_w.shape, F32),
        name="settled",
    )(shared_w, input_grad, own_sum)
    grad_shared_w = jnp.sum(lax.all_gather(shared_w, "tensor", axis=0), axis=0)
    input_grad = assembled(input_grad, pieces, [block_out])
    return (
        block_out.reshape(residual_in.shape),
        input_grad.reshape(residual_in.shape),
        small_in,
        grad_main_w,
        grad_shared_w,
        grad_step_w,
        small_main,
        small_shared,
        small_terms,
        small_out,
        grad_out_w,
    )


def solution(mesh):
    placed = (
        P("dp", "seq", None),
        P("dp"),
        P(),
        P(None, None, "tensor"),
        P(),
        P(None, "tensor"),
        P(None, "tensor"),
        P(),
        P(None, "tensor"),
        P("tensor"),
        P("tensor", None),
        P("dp", "seq", None),
    )
    return jax.shard_map(
        per_device,
        mesh=mesh,
        in_specs=placed,
        out_specs=(
            P("dp", "seq", None),
            P("dp", "seq", None),
            P(),
            P(("seq", "dp"), None, "tensor"),
            P(("seq", "dp"), None),
            P(("seq", "dp"), "tensor"),
            P(None, "tensor"),
            P(),
            P(None, "tensor"),
            P("tensor"),
            P("tensor", ("seq", "dp")),
        ),
        check_vma=False,
    )
```

```python
import functools

import jax
import jax.numpy as jnp
from jax import lax
from jax.experimental import pallas as pl
from jax.experimental.pallas import tpu as pltpu
from jax.sharding import PartitionSpec as P

HEADDIM = 64
CONV = 4
BLOCK_LEN = 256
EPSILON = 1e-05
LOG2E = 1.4426950408889634
LANES = 128
SEG = 16
HALO = 16
VMEM = 60 * 1024 * 1024
STREAMS = 2

F32 = jnp.float32
LOW = jnp.bfloat16


def shifted(block, axis, distance):
    devices = range(lax.axis_size(axis))
    route = [(i - distance, i) for i in devices if i - distance in devices]
    return lax.ppermute(block, axis, route)


def mm(a, b):
    return lax.dot_general(a, b, (((1,), (0,)), ((), ())), preferred_element_type=F32)


def mm_nt(a, b):
    return lax.dot_general(a, b, (((1,), (1,)), ((), ())), preferred_element_type=F32)


def mm_tn(a, b):
    return lax.dot_general(a, b, (((0,), (0,)), ((), ())), preferred_element_type=F32)


def halves(a):
    high = a.astype(LOW)
    return high, (a - high.astype(F32)).astype(LOW)


def sigmoid(v):
    return 0.5 * jnp.tanh(0.5 * v) + 0.5


def lane_of(shape):
    return lax.broadcasted_iota(jnp.int32, shape, 1)


def first_lanes(a, count):
    return jnp.where(lane_of(a.shape) < count, a, 0.0)


def pieces_of(a):
    high = a.astype(LOW).astype(F32)
    rest = a - high
    middle = rest.astype(LOW).astype(F32)
    least = rest - middle
    return (high + pltpu.roll(middle, SEG, 1) + pltpu.roll(least, 2 * SEG, 1)).astype(LOW)


def spread_heads(a, one_hot):
    return mm(pieces_of(a), one_hot)


def sum_heads(a, one_hot_t):
    high, least = halves(a)
    return mm(high, one_hot_t) + mm(least, one_hot_t)


def running_sum(a, triangle, heads):
    p = mm(triangle, pieces_of(a))
    p = p + pltpu.roll(p, LANES - SEG, 1) + pltpu.roll(p, LANES - 2 * SEG, 1)
    return first_lanes(p, heads)


def row_sums(a):
    rows, width = a.shape
    return jnp.sum(a.reshape(rows // 8, 8, width), axis=0)


def lower(extent):
    return lax.broadcasted_iota(jnp.int32, (extent, extent), 0) >= lane_of((extent, extent))


def pair_split(tile):
    first = lane_of(tile.shape) < HEADDIM
    zero = jnp.zeros_like(tile)
    return jnp.where(first, tile, zero), jnp.where(first, zero, tile)


def params(vmem=VMEM):
    return pltpu.CompilerParams(dimension_semantics=("arbitrary",), vmem_limit_bytes=vmem)


def whole(shape):
    return pl.BlockSpec(shape, lambda i: (0,) * len(shape), pipeline_mode=pl.Buffered(1))


def per_seq(*shape, offset=0):
    return pl.BlockSpec((1,) + shape, lambda i: (i + offset,) + (0,) * len(shape))


def project_kernel(
    heads, width, state, block,
    x_ref, halo_ref, gain_ref, main_w, side_w, taps_ref, terms_ref, hot_ref,
    low_ref, mixed_ref, edge_ref, pre_ref, gate_ref, heads_ref, step_ref, y_ref, state_ref, end_ref, through_ref,
    low_scr, mix_scr, k_scr,
):
    rows = x_ref.shape[1]
    gain = gain_ref[...]

    def lowered(x):
        x = x.astype(F32)
        scale = lax.rsqrt(jnp.mean(x * x, axis=1, keepdims=True) + EPSILON)
        return (x * scale * gain).astype(LOW)

    low_scr[:HALO] = lowered(halo_ref[0])
    low_scr[HALO:] = lowered(x_ref[0])
    low_ref[0] = low_scr[HALO:]
    gate_ref[0] = mm(low_scr[HALO:], main_w[:, :width])
    main_in = mm(low_scr[...], main_w[:, width:]).astype(LOW)
    side_in = mm(low_scr[...], side_w[...])
    mix_scr[:, :width] = main_in.astype(F32)
    mix_scr[:, width:] = side_in[:, : 2 * state].astype(LOW).astype(F32)
    mixed_ref[0] = mix_scr[HALO:].astype(LOW)
    edge_ref[0] = mix_scr[:HALO].astype(LOW)
    conv = taps_ref[CONV : CONV + 1]
    for k in range(CONV):
        at = HALO - (CONV - 1) + k
        conv = conv + taps_ref[k : k + 1] * mix_scr[at : at + rows]
    pre_ref[0] = conv
    active = conv * sigmoid(conv)
    step_arg = side_in[HALO:, 2 * state :] + terms_ref[0:1]
    step = jnp.maximum(step_arg, 0.0) + jnp.log1p(jnp.exp(-jnp.abs(step_arg)))
    step = first_lanes(step, heads)
    slope = first_lanes(sigmoid(step_arg), heads)
    decay2 = step * (terms_ref[1:2] * LOG2E)
    hot = hot_ref[...]
    triangle = lower(block).astype(F32).astype(LOW)
    sub = block // 2
    tri_sub = lower(sub)
    k_scr[:, :sub, sub:block] = jnp.zeros((2, sub, sub), LOW)
    k_scr[:, :sub, block + sub :] = jnp.zeros((2, sub, sub), LOW)
    held = None
    for b in range(rows // block):
        span = slice(b * block, (b + 1) * block)
        run = running_sum(decay2[span], triangle, heads)
        heads_ref[0, span] = step[span] + pltpu.roll(run, SEG, 1) + pltpu.roll(slope[span], 2 * SEG, 1)
        last = run[block - 1 : block]
        toward = jnp.exp2(last - run)
        values = active[span, :width]
        stepped = spread_heads(step[span], hot) * values
        step_low = stepped.astype(LOW)
        step_ref[0, span] = step_low
        inject_h, inject_l = halves(active[span, width : width + state])
        readout_h, readout_l = halves(active[span, width + state :])
        meet = mm_nt(readout_h, inject_h) + mm_nt(readout_l, inject_h) + mm_nt(readout_h, inject_l)
        meet_tiles = {
            (0, 0): jnp.where(tri_sub, meet[:sub, :sub], 0.0),
            (1, 0): meet[sub:, :sub],
            (1, 1): jnp.where(tri_sub, meet[sub:, sub:], 0.0),
        }
        run_t = jnp.transpose(run)
        for pair in range(heads // 2):
            slot = pair % 2
            for j in range(2):
                h = 2 * pair + j
                for (r, c), tile in meet_tiles.items():
                    gap = run[r * sub : (r + 1) * sub, h : h + 1] - run_t[h : h + 1, c * sub : (c + 1) * sub]
                    at = j * block + c * sub
                    k_scr[slot, r * sub : (r + 1) * sub, at : at + sub] = (
                        tile * jnp.exp2(jnp.minimum(gap, 0.0))
                    ).astype(LOW)
            lanes = slice(pair * LANES, (pair + 1) * LANES)
            one, two = pair_split(step_low[:, lanes])
            y_ref[0, span, lanes] = mm(k_scr[slot], jnp.concatenate([one, two], axis=0))
        weighed = (spread_heads(first_lanes(toward, heads), hot) * stepped).astype(LOW)
        gained = mm_tn(inject_h, weighed)
        through = spread_heads(first_lanes(jnp.broadcast_to(jnp.exp2(last), (8, LANES)), heads), hot)
        if held is not None:
            gained = gained + held * through[0:1]
            total_through = total_through * through
        else:
            total_through = through
        held = gained
        state_ref[0, b] = held
    end_ref[0] = held
    through_ref[0] = total_through


def gate_kernel(
    heads, width, state, block,
    y_in, pre_ref, gate_ref, heads_ref, state_ref, back_ref, gain_ref, skip_ref, hot_ref, *refs,
):
    y_ref, enter_ref, stats_ref = refs[-3:]
    rows = y_in.shape[1]
    hot = hot_ref[...]
    enter = decayed = sum(ref[0] for ref in refs[:-3])
    enter_ref[0] = enter
    gain = gain_ref[...]
    skip = skip_ref[...]
    for b in range(rows // block):
        span = slice(b * block, (b + 1) * block)
        run = first_lanes(pltpu.roll(heads_ref[0, span], LANES - SEG, 1), heads)
        grown = spread_heads(first_lanes(jnp.exp2(run), heads), hot)
        pre = pre_ref[0, span]
        active = pre * sigmoid(pre)
        readout_h, readout_l = halves(active[:, width + state :])
        enter_h, enter_l = halves(enter)
        carried = mm(readout_h, enter_h) + mm(readout_l, enter_h) + mm(readout_h, enter_l)
        y = y_in[0, span] + grown * carried
        y_ref[0, span] = y
        decayed = decayed * grown[block - 1 : block]
        enter = state_ref[0, b] + decayed
        scanned = y + skip * active[:, :width]
        gate = gate_ref[0, span]
        gated = scanned * (gate * sigmoid(gate))
        squares = jnp.sum(gated * gated, axis=1, keepdims=True)
        inner = jnp.sum(gated * (back_ref[0, span] * gain), axis=1, keepdims=True)
        lane = lane_of((block, LANES))
        stats = jnp.where(lane == 0, squares, jnp.where(lane == 1, inner, 0.0))
        stats_ref[0, :, span] = jnp.transpose(stats)[:8]


def out_kernel(
    heads, width, state, block, inner_total, rank_ref,
    y_ref, pre_ref, gate_ref, heads_ref, back_ref, stats_ref, gain_ref, skip_ref, hot_ref,
    normed_ref, grad_y_ref, grad_gate_ref, adjoint_ref, sums_ref, *out_refs,
):
    rows = y_ref.shape[1]

    @pl.when(pl.program_id(0) == 0)
    def _():
        sums_ref[...] = jnp.zeros_like(sums_ref)

    hot = hot_ref[...]
    gain = gain_ref[...]
    skip = skip_ref[...]
    held = None
    for b in reversed(range(rows // block)):
        span = slice(b * block, (b + 1) * block)
        total = jnp.sum(stats_ref[:, 0, :, span], axis=0)
        total = jnp.transpose(jnp.concatenate([total, jnp.zeros((LANES - 8, block), F32)], axis=0))
        scale = lax.rsqrt(total[:, 0:1] / inner_total + EPSILON)
        bend = scale * scale * scale * (total[:, 1:2] / inner_total)
        pre = pre_ref[0, span]
        active = pre * sigmoid(pre)
        values = active[:, :width]
        scanned = y_ref[0, span] + skip * values
        gate = gate_ref[0, span]
        sig = sigmoid(gate)
        gate_act = gate * sig
        gated = scanned * gate_act
        normed = (gated * scale * gain).astype(LOW)
        normed_ref[0, span] = normed
        back = back_ref[0, span]
        grad_gated = scale * (back * gain) - gated * bend
        grad_y = grad_gated * gate_act
        grad_y_ref[0, span] = grad_y
        grad_gate_ref[0, span] = (grad_gated * scanned * (sig * (1.0 + gate * (1.0 - sig)))).astype(LOW)
        sums_ref[:8] += row_sums(back * gated * scale)
        sums_ref[8:] += row_sums(grad_y * values)
        run = first_lanes(pltpu.roll(heads_ref[0, span], LANES - SEG, 1), heads)
        grown = spread_heads(first_lanes(jnp.exp2(run), heads), hot)
        gained = mm_tn(active[:, width + state :].astype(LOW), (grown * grad_y).astype(LOW))
        if held is not None:
            gained = gained + held * grown[block - 1 : block]
        held = gained
        adjoint_ref[0, b] = held
    by_rank(normed_ref[0], rank_ref[0], out_refs)


def back_kernel(
    heads, width, state, block,
    y_ref, pre_ref, mixed_ref, edge_ref, heads_ref, step_ref, grad_y_ref, enter_ref, state_ref, adjoint_ref,
    taps_ref, terms_ref, skip_ref, hot_ref, hot_t_ref, *refs,
):
    leave_refs, refs = refs[:-10], refs[-10:]
    (
    grad_mixed_ref, grad_step_ref, head_ref, tail_ref, filter_ref, terms_out_ref,
    k_scr, u_scr, cross_scr, conv_scr,
    ) = refs
    rows = y_ref.shape[1]
    blocks = rows // block

    @pl.when(pl.program_id(0) == 0)
    def _():
        filter_ref[...] = jnp.zeros_like(filter_ref)
        terms_out_ref[...] = jnp.zeros_like(terms_out_ref)

    hot = hot_ref[...]
    hot_t = hot_t_ref[...]
    skip = skip_ref[...]
    sub = block // 2
    tri = lower(block)
    upper_sub = jnp.logical_not(lower(sub)) | (
        lax.broadcasted_iota(jnp.int32, (sub, sub), 0) == lane_of((sub, sub))
    )
    upper = jnp.logical_not(tri) | (
        lax.broadcasted_iota(jnp.int32, (block, block), 0) == lane_of((block, block))
    )
    suffix = upper.astype(F32).astype(LOW)
    rate = terms_ref[1:2]
    k_scr[:, sub:, :sub] = jnp.zeros((2, sub, sub), LOW)
    k_scr[:, sub:, block : block + sub] = jnp.zeros((2, sub, sub), LOW)
    conv_scr[:HALO] = jnp.zeros((HALO, conv_scr.shape[1]), F32)
    conv_scr[HALO + rows :] = jnp.zeros((HALO, conv_scr.shape[1]), F32)
    leave = sum(ref[0].astype(F32) for ref in leave_refs)
    runs = [first_lanes(pltpu.roll(heads_ref[0, b * block : (b + 1) * block], LANES - SEG, 1), heads) for b in range(blocks)]
    enters = [enter_ref[0]]
    decayed = enter_ref[0]
    for b in range(blocks):
        last = jnp.broadcast_to(jnp.exp2(runs[b][block - 1 : block]), (8, LANES))
        decayed = decayed * spread_heads(first_lanes(last, heads), hot)[0:1]
        enters.append(state_ref[0, b] + decayed)
    for b in reversed(range(blocks)):
        span = slice(b * block, (b + 1) * block)
        packed = heads_ref[0, span]
        step = first_lanes(packed, heads)
        slope_step = first_lanes(pltpu.roll(packed, LANES - 2 * SEG, 1), heads)
        run = runs[b]
        last = run[block - 1 : block]
        pre = pre_ref[0, span]
        sig = sigmoid(pre)
        active = pre * sig
        slope = sig * (1.0 + pre * (1.0 - sig))
        values = active[:, :width]
        inject_h, inject_l = halves(active[:, width : width + state])
        readout_h, readout_l = halves(active[:, width + state :])
        step_low = step_ref[0, span]
        grad_y = grad_y_ref[0, span]
        grad_low = grad_y.astype(LOW)
        leave_low = leave.astype(LOW)
        toward = spread_heads(first_lanes(jnp.exp2(last - run), heads), hot)
        grown = spread_heads(first_lanes(jnp.exp2(run), heads), hot)
        grown_h, grown_l = halves(grown * grad_y)
        u_scr[...] = toward * mm(inject_h, leave_low)
        meet = mm_nt(inject_h, readout_h) + mm_nt(inject_h, readout_l) + mm_nt(inject_l, readout_h)
        meet_tiles = {
            (0, 0): jnp.where(upper_sub, meet[:sub, :sub], 0.0),
            (0, 1): meet[:sub, sub:],
            (1, 1): jnp.where(upper_sub, meet[sub:, sub:], 0.0),
        }
        run_t = jnp.transpose(run)
        cross_scr[...] = jnp.zeros_like(cross_scr)
        for pair in range(heads // 2):
            slot = pair % 2
            lanes = slice(pair * LANES, (pair + 1) * LANES)
            tile_low = step_low[:, lanes]
            split = pair_split(grad_low[:, lanes])
            for j in range(2):
                h = 2 * pair + j
                products = {}
                top = mm_nt(tile_low[:sub], split[j])
                products[(0, 0)] = top[:, :sub]
                products[(0, 1)] = top[:, sub:]
                products[(1, 1)] = mm_nt(tile_low[sub:], split[j][sub:])
                for (r, c), tile in meet_tiles.items():
                    gap = run_t[h : h + 1, c * sub : (c + 1) * sub] - run[r * sub : (r + 1) * sub, h : h + 1]
                    fall = jnp.exp2(jnp.minimum(gap, 0.0))
                    at = j * block + c * sub
                    k_scr[slot, r * sub : (r + 1) * sub, at : at + sub] = (tile * fall).astype(LOW)
                    cross_scr[r * sub : (r + 1) * sub, c * sub : (c + 1) * sub] += fall * products[(r, c)]
            u_scr[:, lanes] += mm(k_scr[slot], jnp.concatenate(split, axis=0))
        cross = jnp.where(upper, cross_scr[...], 0.0).astype(LOW)
        enter_h, enter_l = halves(enters[b])
        grad_readout = (
            mm_tn(cross, inject_h) + mm_nt(grown_h, enter_h) + mm_nt(grown_l, enter_h) + mm_nt(grown_h, enter_l)
        )
        weighed = (toward * step_low.astype(F32)).astype(LOW)
        grad_inject = mm(cross, readout_h) + mm_nt(weighed, leave_low)
        u = u_scr[...]
        grad_step = sum_heads(values * u, hot_t)
        taken = step_low.astype(F32) * u
        given = grad_low.astype(F32) * y_ref[0, span]
        flow = running_sum(sum_heads(given - taken, hot_t), suffix, heads)
        ends = jnp.sum(leave * enters[b + 1], axis=0, keepdims=True)
        flow = flow + first_lanes(sum_heads(jnp.broadcast_to(ends, (8, width)), hot_t)[0:1], heads)
        grad_arg = (grad_step + rate * flow) * slope_step
        grad_step_ref[0, span] = grad_arg.astype(LOW)
        terms_out_ref[:8] += row_sums(grad_arg)
        terms_out_ref[8:] += row_sums(flow * step * rate)
        grad_values = spread_heads(step, hot) * u + skip * grad_y
        conv_scr[HALO + b * block : HALO + (b + 1) * block, :width] = grad_values * slope[:, :width]
        conv_scr[HALO + b * block : HALO + (b + 1) * block, width : width + state] = (
            grad_inject * slope[:, width : width + state]
        )
        conv_scr[HALO + b * block : HALO + (b + 1) * block, width + state :] = (
            grad_readout * slope[:, width + state :]
        )
        if b:
            leave = adjoint_ref[0, b] + grown[block - 1 : block] * leave
    head_ref[0] = conv_scr[HALO : HALO + 8]
    mixed = mixed_ref[0].astype(F32)
    edge = edge_ref[0].astype(F32)
    total = None
    for k in range(CONV):
        ahead = CONV - 1 - k
        moved = conv_scr[HALO + ahead : HALO + ahead + rows]
        term = taps_ref[k : k + 1] * moved
        total = term if total is None else total + term
        filter_ref[8 * k : 8 * k + 8] += row_sums(mixed * moved) + row_sums(edge * conv_scr[ahead : ahead + HALO])
    filter_ref[8 * CONV :] += row_sums(conv_scr[HALO : HALO + rows])
    high, least = halves(total)
    grad_mixed_ref[0, :, : width + 2 * state] = high
    grad_mixed_ref[0, :, width + 2 * state :] = least[:, width:]
    tail_ref[0] = total[rows - HALO :]


def top_kernel(rows, first, length_ref, place_ref, cot_ref, out_w, top_ref, back_ref):
    valid = length_ref[first + pl.program_id(0)] - place_ref[0]
    cot = cot_ref[0]
    row = lax.broadcasted_iota(jnp.int32, cot.shape, 0)
    top = jnp.where(row < valid, cot.astype(F32), 0.0).astype(LOW)
    top_ref[0] = top
    back_ref[0] = mm_nt(top, out_w[...])


def by_rank(rows, rank, out_refs):
    share = out_refs[0].shape[0]
    count = rows.shape[0] // share
    for k in range(count):
        place = (pl.program_id(0) * count + k) ^ rank
        for d in range(len(out_refs)):

            @pl.when(place == d)
            def _(k=k, d=d):
                out_refs[d][...] = rows[k * share : (k + 1) * share]


def lowered_kernel(width, state, gate_ref, mixed_ref, step_ref, main_w, side_w, out_ref):
    main = jnp.concatenate([gate_ref[0], mixed_ref[0, :, :width]], axis=1)
    side = jnp.concatenate([mixed_ref[0, :, width : width + 2 * state], step_ref[0]], axis=1)
    out_ref[0] = (mm_nt(main, main_w[...]) + mm_nt(side, side_w[...])).astype(LOW)


def product_kernel(ranks, rank_ref, *refs):
    x_refs, weight_ref = refs[:STREAMS], refs[STREAMS]
    parts = refs[STREAMS + 1 : -2]
    out_ref, acc_ref = refs[-2:]
    share = parts[0].shape[0]
    at = pl.program_id(0)
    for d in range(ranks):

        @pl.when(at == d)
        def _(d=d):
            rows = jnp.concatenate([parts[s * ranks + d][...] for s in range(STREAMS)], axis=0)
            part = mm(rows, weight_ref[0])
            if d == 0:
                part = part + jnp.concatenate([x[0].astype(F32) for x in x_refs], axis=0)
            else:
                part = part + acc_ref[...]
            acc_ref[...] = part

    @pl.when(at == ranks - 1)
    def _():
        for s in range(STREAMS):
            out_ref[s] = acc_ref[s * share : (s + 1) * share].astype(LOW)


def hand_kernel(local_ref, through_ref, arrived_ref, out_ref):
    out_ref[0] = local_ref[0] + through_ref[0, :1] * arrived_ref[0]


def place_kernel(block_ref, out_ref):
    out_ref[...] = block_ref[...]


def settle_kernel(wide_ref, rest_ref, out_ref):
    rows, width = wide_ref.shape
    groups = width // LANES
    for k in range(groups):
        out_ref[k * rows : (k + 1) * rows] = wide_ref[:, k * LANES : (k + 1) * LANES]
    out_ref[groups * rows :] = rest_ref[...]


def merged(ref):
    return ref[...].reshape(ref.shape[0] * ref.shape[1], ref.shape[2])


def lane_sums(a):
    return sum(a[:, k : k + LANES] for k in range(0, a.shape[1], LANES))


def gate_grad_kernel(*refs):
    low, grads = refs[:STREAMS], refs[STREAMS : 2 * STREAMS]
    main_w, out_ref, gain_ref = refs[2 * STREAMS :]
    gate = sum(mm_tn(merged(a), merged(b)) for a, b in zip(low, grads))
    out_ref[...] = gate.astype(LOW)
    gain_ref[...] = lane_sums(main_w[...].astype(F32) * gate)


def out_grad_kernel(*refs):
    top, normed, out_ref = refs[:STREAMS], refs[STREAMS : 2 * STREAMS], refs[-1]
    out_ref[...] = sum(mm_tn(merged(a), merged(b)) for a, b in zip(top, normed)).astype(LOW)


def late_kernel(width, state, *refs):
    low, mixed, step = (refs[k * STREAMS : (k + 1) * STREAMS] for k in range(3))
    main_w, side_w, gain_in, own_ref, shared_ref, gain_ref = refs[3 * STREAMS :]
    total = sum(mm_tn(merged(a), merged(b)) for a, b in zip(low, mixed))
    steps = sum(mm_tn(merged(a), merged(b)) for a, b in zip(low, step))
    main = total[:, :width]
    shared = total[:, width : width + 2 * state] + total[:, width + 2 * state :]
    own_ref[:, :width] = main.astype(LOW)
    own_ref[:, width:] = steps.astype(LOW)
    shared_ref[...] = shared
    side = side_w[...].astype(F32)
    gain_ref[...] = (
        gain_in[...]
        + lane_sums(main_w[...].astype(F32) * main)
        + lane_sums(side[:, : 2 * state] * shared)
        + side[:, 2 * state :] * steps
    )


def by_rank(rows, rank, out_refs):
    share = out_refs[0].shape[0]
    count = rows.shape[0] // share
    for k in range(count):
        place = (pl.program_id(0) * count + k) ^ rank
        for d in range(len(out_refs)):

            @pl.when(place == d)
            def _(k=k, d=d):
                out_refs[d][...] = rows[k * share : (k + 1) * share]


def lowered_kernel(width, state, rank_ref, gate_ref, mixed_ref, step_ref, main_w, side_w, *out_refs):
    main = jnp.concatenate([gate_ref[0], mixed_ref[0, :, :width]], axis=1)
    side = jnp.concatenate([mixed_ref[0, :, width : width + 2 * state], step_ref[0]], axis=1)
    total = (mm_nt(main, main_w[...]) + mm_nt(side, side_w[...])).astype(LOW)
    by_rank(total, rank_ref[0], out_refs)


def norm_kernel(ranks, rank_ref, x_ref, top_ref, gain_ref, *refs):
    out_ref = refs[ranks]
    x = x_ref[0].astype(F32)
    scale = lax.rsqrt(jnp.mean(x * x, axis=1, keepdims=True) + EPSILON)
    normed = x * scale
    grad = sum(ref[...].astype(F32) for ref in refs[:ranks])
    scaled = grad * gain_ref[...]
    out = top_ref[0].astype(F32) + scale * (scaled - normed * jnp.mean(scaled * normed, axis=1, keepdims=True))
    out_ref[...] = out.astype(LOW)


def ignoring(kernel, first, count):
    def body(*refs):
        kernel(*refs[:first], *refs[first + count :])

    return body


def per_device(
    residual_in,
    lengths,
    input_gain,
    main_in_weight,
    weight_shared,
    step_in_weight,
    filter_main,
    filter_shared,
    head_terms,
    output_gain,
    out_projection_weight,
    cotangent,
):
    all_seqs, rows, model = residual_in.shape
    seqs = all_seqs // STREAMS
    heads = step_in_weight.shape[1]
    width = main_in_weight.shape[2]
    state = weight_shared.shape[1] // 2
    mixed_width = width + 2 * state
    kept_width = mixed_width + 2 * state
    ranks = lax.axis_size("tensor")
    spans = lax.axis_size("seq")
    inner_total = width * ranks
    reach = CONV - 1
    block = min(BLOCK_LEN, rows)
    blocks = rows // block
    share = seqs * rows // ranks
    sds = jax.ShapeDtypeStruct

    main_w = main_in_weight.reshape(model, 2 * width)
    side_w = jnp.concatenate(
        [weight_shared, jnp.pad(step_in_weight, ((0, 0), (0, LANES - heads)))], axis=1
    )
    side_width = side_w.shape[1]
    taps = jnp.pad(jnp.concatenate([filter_main, filter_shared], axis=1), ((0, 8 - CONV - 1), (0, 0)))
    rate = -jnp.exp(head_terms[1])
    terms = jnp.pad(jnp.stack([head_terms[0], rate]), ((0, 6), (0, LANES - heads)))
    skip = jnp.repeat(head_terms[2], HEADDIM)[None]
    channel_head = jnp.arange(width, dtype=jnp.int32)[None, :] // HEADDIM
    lane = jnp.arange(LANES, dtype=jnp.int32)[:, None]
    hot = ((lane % SEG == channel_head) & (lane < 3 * SEG)).astype(LOW)
    hot_t = (lane == channel_head).astype(LOW).T
    in_gain = input_gain[None]
    out_gain = output_gain[None]
    dims = (heads, width, state, block)
    place = (lax.axis_index("seq") * rows).astype(jnp.int32)[None]
    rank = lax.axis_index("tensor").astype(jnp.int32)[None]
    halo = shifted(residual_in[:, rows - HALO :, :], "seq", 1)
    full_w = lax.all_gather(out_projection_weight, "tensor", axis=0)
    smem = pl.BlockSpec(memory_space=pltpu.SMEM)
    anywhere = pl.BlockSpec(memory_space=pl.ANY)

    def cost(flops):
        return pl.CostEstimate(flops=int(flops), bytes_accessed=30 << 20, transcendentals=0)

    def project(s, halo, marks=()):
        return pl.pallas_call(
            ignoring(functools.partial(project_kernel, *dims), 8, len(marks)),
            grid=(seqs,),
            in_specs=[
                per_seq(rows, model, offset=s * seqs), per_seq(HALO, model, offset=s * seqs), whole((1, model)),
                whole((model, 2 * width)), whole((model, side_width)), whole((8, mixed_width)), whole((8, LANES)),
                whole((LANES, width)),
            ]
            + [anywhere] * len(marks),
            out_specs=[
                per_seq(rows, model), per_seq(rows, mixed_width), per_seq(HALO, mixed_width),
                per_seq(rows, mixed_width), per_seq(rows, width), per_seq(rows, LANES), per_seq(rows, width),
                per_seq(rows, width), per_seq(blocks, state, width), per_seq(state, width), per_seq(8, width),
            ],
            out_shape=[
                sds((seqs, rows, model), LOW), sds((seqs, rows, mixed_width), LOW),
                sds((seqs, HALO, mixed_width), LOW), sds((seqs, rows, mixed_width), F32),
                sds((seqs, rows, width), F32), sds((seqs, rows, LANES), F32), sds((seqs, rows, width), LOW),
                sds((seqs, rows, width), F32), sds((seqs, blocks, state, width), F32),
                sds((seqs, state, width), F32), sds((seqs, 8, width), F32),
            ],
            scratch_shapes=[
                pltpu.VMEM((HALO + rows, model), LOW), pltpu.VMEM((HALO + rows, mixed_width), F32),
                pltpu.VMEM((2, block, 2 * block), LOW),
            ],
            compiler_params=params(),
            cost_estimate=cost(8e9 * seqs),
            name="project",
        )(residual_in, halo, in_gain, main_w, side_w, taps, terms, hot, *marks)

    def handed(local, through, arrived, marks):
        return pl.pallas_call(
            ignoring(hand_kernel, 3, len(marks)),
            grid=(seqs,),
            in_specs=[per_seq(state, width), per_seq(8, width), per_seq(state, width)] + [anywhere] * len(marks),
            out_specs=per_seq(state, width),
            out_shape=sds((seqs, state, width), F32),
            compiler_params=params(),
            name="handed",
        )(local, through, arrived, *marks)

    def chained(local, through, direction, kind, marks=None):
        arrivals = []
        for hop in range(spans - 1):
            sender = hop if direction > 0 else spans - 1 - hop
            if hop == 0:
                sent = local
            elif marks:
                sent = handed(local, through, arrivals[-1], marks[min(hop, len(marks)) - 1])
            else:
                sent = local + through[:, :1] * arrivals[-1].astype(F32)
            arrivals.append(lax.ppermute(sent.astype(kind), "seq", [(sender, sender + direction)]))
        return arrivals

    def top_of(s, place, marks=()):
        return pl.pallas_call(
            ignoring(functools.partial(top_kernel, rows, s * seqs), 4, len(marks)),
            grid=(seqs,),
            in_specs=[smem, smem, per_seq(rows, model, offset=s * seqs), whole((width, model))]
            + [anywhere] * len(marks),
            out_specs=[per_seq(rows, model), per_seq(rows, width)],
            out_shape=[sds((seqs, rows, model), LOW), sds((seqs, rows, width), F32)],
            compiler_params=params(),
            cost_estimate=cost(2.5e9 * seqs),
            name="top",
        )(lengths, place, cotangent, out_projection_weight, *marks)

    def gated_of(y_local, pre, gate, packed, arrivals, states, back, marks=()):
        return pl.pallas_call(
            ignoring(functools.partial(gate_kernel, *dims), 9 + len(arrivals), len(marks)),
            grid=(seqs,),
            in_specs=[
                per_seq(rows, width), per_seq(rows, mixed_width), per_seq(rows, width), per_seq(rows, LANES),
                per_seq(blocks, state, width), per_seq(rows, width), whole((1, width)),
                whole((1, width)), whole((LANES, width)),
            ]
            + [per_seq(state, width)] * len(arrivals)
            + [anywhere] * len(marks),
            out_specs=[per_seq(rows, width), per_seq(state, width), per_seq(8, rows)],
            out_shape=[sds((seqs, rows, width), F32), sds((seqs, state, width), F32), sds((seqs, 8, rows), F32)],
            compiler_params=params(),
            cost_estimate=cost(4e9 * seqs),
            name="gated",
        )(y_local, pre, gate, packed, states, back, out_gain, skip, hot, *arrivals, *marks)

    def outward(y, pre, gate, packed, back, all_stats, marks=()):
        seq = lambda *shape: pl.BlockSpec((1,) + shape, lambda i, r: (i,) + (0,) * len(shape))
        fixed = lambda *shape: pl.BlockSpec(shape, lambda i, r: (0,) * len(shape))
        return pl.pallas_call(
            ignoring(functools.partial(out_kernel, *dims, inner_total), 10, len(marks)),
            grid_spec=pltpu.PrefetchScalarGridSpec(
                num_scalar_prefetch=1,
                grid=(seqs,),
                in_specs=[
                    seq(rows, width), seq(rows, mixed_width), seq(rows, width), seq(rows, LANES), seq(rows, width),
                    pl.BlockSpec((ranks, 1, 8, rows), lambda i, r: (0, i, 0, 0)), fixed(1, width), fixed(1, width),
                    fixed(LANES, width),
                ]
                + [anywhere] * len(marks),
                out_specs=[
                    seq(rows, width), seq(rows, width), seq(rows, width), seq(blocks, state, width), fixed(16, width),
                ]
                + [fixed(share, width)] * ranks,
            ),
            out_shape=[
                sds((seqs, rows, width), LOW), sds((seqs, rows, width), F32), sds((seqs, rows, width), LOW),
                sds((seqs, blocks, state, width), F32), sds((16, width), F32),
            ]
            + [sds((share, width), LOW)] * ranks,
            compiler_params=params(),
            cost_estimate=cost(5e9 * seqs),
            name="outward",
        )(rank, y, pre, gate, packed, back, all_stats, out_gain, skip, hot, *marks)

    def backward(marks, y, pre, mixed, edge, packed, stepped, grad_y, entering, states, leaving, adjoint):
        return pl.pallas_call(
            ignoring(functools.partial(back_kernel, *dims), 15 + len(leaving), len(marks)),
            grid=(seqs,),
            in_specs=[
                per_seq(rows, width), per_seq(rows, mixed_width), per_seq(rows, mixed_width),
                per_seq(HALO, mixed_width), per_seq(rows, LANES), per_seq(rows, width), per_seq(rows, width),
                per_seq(state, width), per_seq(blocks, state, width),
                per_seq(blocks, state, width), whole((8, mixed_width)), whole((8, LANES)), whole((1, width)),
                whole((LANES, width)), whole((width, LANES)),
            ]
            + [per_seq(state, width)] * len(leaving)
            + [anywhere] * len(marks),
            out_specs=[
                per_seq(rows, kept_width), per_seq(rows, LANES), per_seq(8, mixed_width), per_seq(HALO, mixed_width),
                pl.BlockSpec((8 * (CONV + 1), mixed_width), lambda i: (0, 0)),
                pl.BlockSpec((16, LANES), lambda i: (0, 0)),
            ],
            out_shape=[
                sds((seqs, rows, kept_width), LOW), sds((seqs, rows, LANES), LOW), sds((seqs, 8, mixed_width), F32),
                sds((seqs, HALO, mixed_width), F32), sds((8 * (CONV + 1), mixed_width), F32), sds((16, LANES), F32),
            ],
            scratch_shapes=[
                pltpu.VMEM((2, block, 2 * block), LOW), pltpu.VMEM((block, width), F32),
                pltpu.VMEM((block, block), F32), pltpu.VMEM((2 * HALO + rows, mixed_width), F32),
            ],
            compiler_params=params(),
            cost_estimate=cost(11e9 * seqs),
            name="backward",
        )(
            y, pre, mixed, edge, packed, stepped, grad_y, entering, states, adjoint,
            taps, terms, skip, hot, hot_t, *leaving, *marks,
        )

    def lowered_of(grad_gate, grad_mixed, grad_step, marks=()):
        seq = lambda *shape: pl.BlockSpec((1,) + shape, lambda i, r: (i,) + (0,) * len(shape))
        fixed = lambda *shape: pl.BlockSpec(shape, lambda i, r: (0,) * len(shape), pipeline_mode=pl.Buffered(1))
        return pl.pallas_call(
            ignoring(functools.partial(lowered_kernel, width, state), 6, len(marks)),
            grid_spec=pltpu.PrefetchScalarGridSpec(
                num_scalar_prefetch=1,
                grid=(seqs,),
                in_specs=[
                    seq(rows, width), seq(rows, kept_width), seq(rows, LANES), fixed(model, 2 * width),
                    fixed(model, side_width),
                ]
                + [anywhere] * len(marks),
                out_specs=[pl.BlockSpec((share, model), lambda i, r: (0, 0))] * ranks,
            ),
            out_shape=[sds((share, model), LOW)] * ranks,
            compiler_params=params(),
            cost_estimate=cost(4.5e9 * seqs),
            name="lowered",
        )(rank, grad_gate, grad_mixed, grad_step, main_w, side_w, *marks)

    def input_norm(s, parts, top, marks=()):
        return pl.pallas_call(
            ignoring(functools.partial(norm_kernel, ranks), 4 + len(parts), len(marks)),
            grid_spec=pltpu.PrefetchScalarGridSpec(
                num_scalar_prefetch=1,
                grid=(1,),
                in_specs=[
                    pl.BlockSpec((1, share, model), lambda i, r: (s * ranks + r[0], 0, 0)),
                    pl.BlockSpec((1, share, model), lambda i, r: (r[0], 0, 0)),
                    pl.BlockSpec((1, model), lambda i, r: (0, 0)),
                ]
                + [pl.BlockSpec((share, model), lambda i, r: (0, 0))] * ranks
                + [anywhere] * len(marks),
                out_specs=pl.BlockSpec((share, model), lambda i, r: (0, 0)),
            ),
            out_shape=sds((share, model), LOW),
            compiler_params=params(),
            name="input_norm",
        )(rank, residual_in.reshape(-1, share, model), top.reshape(-1, share, model), in_gain, *parts, *marks)

    def product(parts, marks=()):
        row_of = lambda s: pl.BlockSpec((1, share, model), lambda i, r: (s * ranks + r[0], 0, 0))
        x = residual_in.reshape(-1, share, model)
        return pl.pallas_call(
            ignoring(functools.partial(product_kernel, ranks), 2 + STREAMS + len(parts), len(marks)),
            grid_spec=pltpu.PrefetchScalarGridSpec(
                num_scalar_prefetch=1,
                grid=(ranks,),
                in_specs=[row_of(s) for s in range(STREAMS)]
                + [pl.BlockSpec((1, width, model), lambda i, r: (r[0] ^ i, 0, 0))]
                + [pl.BlockSpec((share, width), lambda i, r: (0, 0))] * (STREAMS * ranks)
                + [anywhere] * len(marks),
                out_specs=pl.BlockSpec((STREAMS, share, model), lambda i, r: (0, 0, 0)),
                scratch_shapes=[pltpu.VMEM((STREAMS * share, model), F32)],
            ),
            out_shape=sds((STREAMS, share, model), LOW),
            compiler_params=params(),
            cost_estimate=cost(2.4e9 * all_seqs),
            name="product",
        )(rank, *[x] * STREAMS, full_w, *parts, *marks)

    tile = 256
    tiles = model // tile
    column = pl.BlockSpec((seqs, rows, tile), lambda i: (0, 0, i))
    row = lambda n: pl.BlockSpec((tile, n), lambda i: (i, 0))

    def gate_grad(low, grads, marks=()):
        return pl.pallas_call(
            ignoring(gate_grad_kernel, 2 * STREAMS + 1, len(marks)),
            grid=(tiles,),
            in_specs=[column] * STREAMS + [whole((seqs, rows, width))] * STREAMS + [row(width)]
            + [anywhere] * len(marks),
            out_specs=[row(width), row(LANES)],
            out_shape=[sds((model, width), LOW), sds((model, LANES), F32)],
            compiler_params=params(),
            cost_estimate=cost(2.5e9 * all_seqs),
            name="gate_grad",
        )(*low, *grads, main_w, *marks)

    def out_grad(top, normed, marks=()):
        return pl.pallas_call(
            ignoring(out_grad_kernel, 2 * STREAMS, len(marks)),
            grid=(tiles,),
            in_specs=[column] * STREAMS + [whole((seqs, rows, width))] * STREAMS + [anywhere] * len(marks),
            out_specs=row(width),
            out_shape=sds((model, width), LOW),
            compiler_params=params(),
            cost_estimate=cost(2.5e9 * all_seqs),
            name="out_grad",
        )(*top, *normed, *marks)

    def late_of(low, mixed, step, gain, marks=()):
        return pl.pallas_call(
            ignoring(functools.partial(late_kernel, width, state), 3 * STREAMS + 3, len(marks)),
            grid=(tiles,),
            in_specs=[column] * STREAMS
            + [whole((seqs, rows, kept_width))] * STREAMS
            + [whole((seqs, rows, LANES))] * STREAMS
            + [pl.BlockSpec((tile, width), lambda i: (i, 1)), row(side_width), row(LANES)]
            + [anywhere] * len(marks),
            out_specs=[row(width + LANES), row(2 * state), row(LANES)],
            out_shape=[sds((model, width + LANES), LOW), sds((model, 2 * state), F32), sds((model, LANES), F32)],
            compiler_params=params(),
            cost_estimate=cost(5e9 * all_seqs),
            name="late",
        )(*low, *mixed, *step, main_w, side_w, gain, *marks)

    def exchanged(own):
        return [own] + [
            lax.ppermute(own, "tensor", [(i, i ^ d) for i in range(ranks)]) for d in range(1, ranks)
        ]

    def swapped(blocks_of):
        return [
            lax.ppermute(b, "tensor", [(i, i ^ d) for i in range(ranks)]) if d else b for d, b in enumerate(blocks_of)
        ]

    def scattered(whole_rows):
        blocks_of = whole_rows.reshape(ranks, share, -1)
        return swapped([lax.dynamic_index_in_dim(blocks_of, rank[0] ^ d, axis=0, keepdims=False) for d in range(ranks)])

    def placed(blocks, total, marks):
        count = blocks.shape[0]
        return pl.pallas_call(
            ignoring(place_kernel, 1, len(marks)),
            grid=(count // 2,),
            in_specs=[pl.BlockSpec((2, share, model), lambda i: (i, 0, 0))] + [anywhere] * len(marks),
            out_specs=pl.BlockSpec((2, share, model), lambda i: (i, 0, 0)),
            out_shape=sds((total, share, model), LOW),
            compiler_params=params(),
            name="placed",
        )(blocks, *marks)

    def assembled(held, pieces, marks):
        total = held.shape[0]

        def kernel(rank_ref, held_ref, *refs):
            out_ref, sems = refs[ranks:]
            copies = [
                pltpu.make_async_copy(refs[d], out_ref.at[total - ranks + (rank_ref[0] ^ d)], sems.at[d])
                for d in range(ranks)
            ]
            for copy in copies:
                copy.start()
            for copy in copies:
                copy.wait()

        return pl.pallas_call(
            ignoring(kernel, 2 + ranks, len(marks)),
            in_specs=[smem, anywhere] + [pl.BlockSpec(memory_space=pltpu.VMEM)] * ranks + [anywhere] * len(marks),
            out_specs=anywhere,
            out_shape=sds((total, share, model), LOW),
            input_output_aliases={1: 0},
            scratch_shapes=[pltpu.SemaphoreType.DMA((ranks,))],
            compiler_params=pltpu.CompilerParams(vmem_limit_bytes=VMEM),
            name="assemble",
        )(rank, held, *pieces, *marks)

    flat = lambda a: a.reshape(seqs * rows, a.shape[-1])
    both = range(STREAMS)

    def backward_of(s, leaving, marks, fill):
        made, step_low, head, tail, filter_sum, term_sum = backward(
            marks, y[s], pre[s], mixed[s], edge[s], packed[s], stepped[s], grad_y[s], entering[s], states[s],
            leaving, adjoint[s],
        )
        following = shifted(head[:, :reach], "seq", -1)
        fill(step_low)
        fix = jnp.zeros((seqs, reach, mixed_width), F32)
        for k in range(reach):
            fix = fix + jnp.pad(taps[k] * following[:, : reach - k], ((0, 0), (k, 0), (0, 0)))
        tail = tail + jnp.pad(fix, ((0, 0), (HALO - reach, 0), (0, 0)))
        tail_high = tail.astype(LOW)
        tail_least = (tail - lax.optimization_barrier(tail_high).astype(F32)).astype(LOW)[:, :, width:]
        made = lax.dynamic_update_slice(
            made, jnp.concatenate([tail_high, tail_least], axis=2), (0, rows - HALO, 0)
        )
        return made, step_low, filter_sum, term_sum

    reduced = lambda a: lax.psum_scatter(a, ("seq", "dp"), scatter_dimension=0, tiled=True)

    first = [project(0, halo)]
    first.append(project(1, halo, [first[0][-1]]))
    low, mixed, edge, pre, gate, packed, stepped, y_local, states, local, through = zip(*first)
    tops = [top_of(0, place, [through[1]])]
    tops.append(top_of(1, place, [tops[0][0]]))
    top, back = zip(*tops)

    def gated_of_stream(s, arrivals, marks):
        y, entering, stats = gated_of(y_local[s], pre[s], gate[s], packed[s], arrivals, states[s], back[s], marks)
        return y, entering, stats, lax.all_gather(stats, "tensor", axis=0)

    y, entering, stats, all_stats = [None] * 2, [None] * 2, [None] * 2, [None] * 2
    second = []
    arrivals = chained(local[0], through[0], 1, F32)
    y[0], entering[0], stats[0], all_stats[0] = gated_of_stream(0, arrivals, [top[1]])
    second.append(outward(y[0], pre[0], gate[0], packed[0], back[0], all_stats[0]))
    arrivals = chained(local[1], through[1], 1, F32)
    y[1], entering[1], stats[1], all_stats[1] = gated_of_stream(1, arrivals, [second[0][0]])
    parts = swapped(second[0][5:])
    leaving = [chained(second[0][3][:, 0], through[0], -1, LOW)]
    second.append(outward(y[1], pre[1], gate[1], packed[1], back[1], all_stats[1], [leaving[0][0]]))
    normed, grad_y, grad_gate, adjoint, out_sums = list(zip(*second))[:5]
    leaving.append(chained(adjoint[1][:, 0], through[1], -1, LOW))
    gate_w, gain_sums = gate_grad(low, grad_gate, [normed[1], leaving[0][1]])
    gate_w_sum = reduced(gate_w)
    made_out = product(parts + swapped(second[1][5:]), [gate_w, leaving[1][0]])
    block_out = lax.all_gather(made_out, "tensor", axis=1, tiled=True)
    out_w = []
    third = [
        backward_of(0, leaving[0], [made_out, leaving[1][1]], lambda raw: out_w.append(out_grad(top, normed, [raw])))
    ]
    out_w_sum = reduced(out_w[0])
    partial = [lowered_of(grad_gate[0], *third[0][:2], [out_w[0]])]
    sums = [swapped(partial[0])]
    own = []
    third.append(
        backward_of(
            1, leaving[1], [partial[0][0]], lambda raw: own.append(input_norm(0, sums[0], top[0], [raw, block_out]))
        )
    )
    first_in = lax.all_gather(own[0], "tensor", axis=0, tiled=True)
    grad_mixed, grad_step, filter_sums, term_sums = zip(*third)
    partial.append(lowered_of(grad_gate[1], *third[1][:2], [own[0], gate_w_sum]))
    grad_own, grad_side, gain_sums = late_of(low, grad_mixed, grad_step, gain_sums, [own[0], partial[1][0]])
    sums.append(swapped(partial[1]))
    own_sum = reduced(grad_own)
    grad_own_w = own_sum.astype(F32)
    shared_w = reduced(grad_side)
    grad_gate_w = gate_w_sum.astype(F32)
    grad_out_w = out_w_sum.astype(F32).T
    grad_main_w = jnp.stack([grad_gate_w, grad_own_w[:, :width]], axis=1)
    grad_step_w = grad_own_w[:, width : width + heads]
    filters = jnp.sum(sum(filter_sums).reshape(CONV + 1, 8, mixed_width), axis=1)
    term_rows = jnp.sum(sum(term_sums).reshape(2, 8, LANES), axis=1)
    out_rows = jnp.sum(sum(out_sums).reshape(2, 8, width), axis=1)
    grad_skip = jnp.pad(jnp.sum(out_rows[1].reshape(heads, HEADDIM), axis=1), (0, LANES - heads))
    everywhere = (jnp.sum(gain_sums, axis=1) / input_gain, filters[:, width:])
    per_rank = (filters[:, :width], jnp.concatenate([term_rows, grad_skip[None]], axis=0), out_rows[0])
    packed_sums = jnp.concatenate([a.reshape(-1) for a in everywhere + per_rank])
    packed_sums = jnp.sum(lax.all_gather(packed_sums.reshape(-1, LANES), ("seq", "dp"), axis=0), axis=0)
    split = (everywhere[0].size + everywhere[1].size) // LANES
    rank_sums = packed_sums[split:].reshape(-1)
    small_main = rank_sums[: (CONV + 1) * width].reshape(CONV + 1, width)
    small_terms = rank_sums[(CONV + 1) * width : -width].reshape(3, LANES)[:, :heads]
    small_out = rank_sums[-width:]
    last_own = input_norm(1, sums[1], top[1], [packed_sums, first_in])
    pieces = exchanged(last_own)
    stacked = STREAMS * ranks
    block_out = placed(block_out.reshape(stacked, share, model), stacked, [last_own])
    input_grad = placed(first_in.reshape(-1, share, model), stacked, [last_own, block_out])
    padded_split = -(-split // 8) * 8
    settled = pl.pallas_call(
        ignoring(settle_kernel, 2, 2),
        in_specs=[pl.BlockSpec(memory_space=pltpu.VMEM)] * 2 + [anywhere] * 2,
        out_specs=pl.BlockSpec(memory_space=pltpu.VMEM),
        out_shape=sds((shared_w.size // LANES + padded_split, LANES), F32),
        name="settled",
    )(shared_w, jnp.pad(packed_sums[:split], ((0, padded_split - split), (0, 0))), input_grad, own_sum)
    settled = jnp.sum(lax.all_gather(settled, "tensor", axis=0), axis=0)
    share_rows = shared_w.shape[0]
    grad_shared_w = jnp.concatenate(
        [settled[k * share_rows : (k + 1) * share_rows] for k in range(2 * state // LANES)], axis=1
    )
    shared_sums = settled[shared_w.size // LANES :][:split].reshape(-1)
    small_in = shared_sums[:model]
    small_shared = shared_sums[model:].reshape(CONV + 1, 2 * state)
    input_grad = assembled(input_grad, pieces, [block_out])
    return (
        block_out.reshape(residual_in.shape),
        input_grad.reshape(residual_in.shape),
        small_in,
        grad_main_w,
        grad_shared_w,
        grad_step_w,
        small_main,
        small_shared,
        small_terms,
        small_out,
        grad_out_w,
    )


def solution(mesh):
    placed = (
        P("dp", "seq", None),
        P("dp"),
        P(),
        P(None, None, "tensor"),
        P(),
        P(None, "tensor"),
        P(None, "tensor"),
        P(),
        P(None, "tensor"),
        P("tensor"),
        P("tensor", None),
        P("dp", "seq", None),
    )
    return jax.shard_map(
        per_device,
        mesh=mesh,
        in_specs=placed,
        out_specs=(
            P("dp", "seq", None),
            P("dp", "seq", None),
            P(),
            P(("seq", "dp"), None, "tensor"),
            P(("seq", "dp"), None),
            P(("seq", "dp"), "tensor"),
            P(None, "tensor"),
            P(),
            P(None, "tensor"),
            P("tensor"),
            P("tensor", ("seq", "dp")),
        ),
        check_vma=False,
    )
```
